512 devices in a mesh: dp: 64 (over z, x), tensor: 8 (over y, core).
Axes of the slice: x: 4, y: 4, z: 16, core: 2. Of those that a mesh axis runs over, the one named last changes fastest.
Arguments:
- grad: bfloat16 [16, 512, 16384], P(None, 'dp', 'tensor'), may hold values from -40 to 40
- owner: int32 [16, 32], replicated, may hold values from 0 to 63, as said below
- left_root: bfloat16 [8, 192, 512, 512], P('tensor', 'dp'), may hold values from -0.5 to 4.5
- right_root: bfloat16 [8, 192, 512, 512], P('tensor', 'dp'), may hold values from -0.5 to 4.5
Outputs:
- direction: bfloat16 [16, 512, 16384], P(None, 'dp', 'tensor')
- update_rms: float32 [], replicated
The draws below stay inside these ranges and needn't reach their ends.
Inputs may be any that keep to these rules, and one draw needn't show every extreme that they name: `owner`: among the 16 x 4 blocks of each tensor index, no dp index owns more than 3, and some dp index owns exactly 3.
All inputs are finite; a program needn't handle non-finite values.
Results may differ from the reference program's by a relative error of at most 0.0049.
Values may be sent and summed in bfloat16 or wider, within the bound.
A program may use at most 64 MiB of HBM per device.

```python
import math
import jax
import jax.numpy as jnp
from jax import lax

BLK = 512
CB = 4
SLOTS = 3
NBR = 16
NBC = 32
ROWS = 8192
COLS = 16384
FSLOTS = 192
N_DP = 64
N_TENSOR = 8


def draw_grad(key, part):
    key = jax.random.fold_in(key, 5)
    key_rows, key_cols, key_vals = jax.random.split(key, 3)
    shape = (NBR, BLK, COLS)
    rows = jnp.exp(jax.random.uniform(key_rows, (NBR, BLK, 1), jnp.float32, 0.0, math.log(10.0)))
    cols = jnp.exp(jax.random.uniform(key_cols, (1, 1, COLS), jnp.float32, 0.0, math.log(10.0)))
    values = jax.random.truncated_normal(key_vals, -4.0, 4.0, shape, jnp.float32)
    return (0.05 * rows * cols * values).astype(jnp.bfloat16)


def draw_owner(key, part):
    key = jax.random.fold_in(key, 11)
    per_group = NBR * CB
    capacity = N_DP * SLOTS

    def one_group(group_key):
        key_perm, key_shift, key_order = jax.random.split(group_key, 3)
        shuffled = jax.random.permutation(key_perm, capacity)
        order = jnp.argsort(jnp.where(shuffled < SLOTS, 0, 1), stable=True)
        chosen = shuffled[order][:per_group]
        offset = jax.random.randint(key_shift, (), 0, N_DP)
        owners = (chosen // SLOTS + offset) % N_DP
        owners = jax.random.permutation(key_order, owners)
        return owners.reshape(NBR, CB)
    groups = jax.vmap(one_group)(jax.random.split(key, N_TENSOR))
    return groups.transpose(1, 0, 2).reshape(NBR, NBC).astype(jnp.int32)


def draw_left_root(key, part):
    key = jax.random.fold_in(key, 17)
    key_noise, key_diag = jax.random.split(key)
    shape = (N_TENSOR, FSLOTS, BLK, BLK)
    noise = jax.random.truncated_normal(key_noise, -4.0, 4.0, shape, jnp.float32) * (0.6 / math.sqrt(BLK))
    diagonal = jnp.exp(jax.random.uniform(key_diag, (N_TENSOR, FSLOTS, BLK, 1), jnp.float32, math.log(1.5), math.log(3.0)))
    identity = (jnp.arange(BLK)[:, None] == jnp.arange(BLK)[None, :]).astype(jnp.float32)
    return (noise + identity * diagonal).astype(jnp.bfloat16)


def draw_right_root(key, part):
    key = jax.random.fold_in(key, 23)
    key_noise, key_diag = jax.random.split(key)
    shape = (N_TENSOR, FSLOTS, BLK, BLK)
    noise = jax.random.truncated_normal(key_noise, -4.0, 4.0, shape, jnp.float32) * (0.6 / math.sqrt(BLK))
    diagonal = jnp.exp(jax.random.uniform(key_diag, (N_TENSOR, FSLOTS, BLK, 1), jnp.float32, math.log(1.5), math.log(3.0)))
    identity = (jnp.arange(BLK)[:, None] == jnp.arange(BLK)[None, :]).astype(jnp.float32)
    return (noise + identity * diagonal).astype(jnp.bfloat16)


def setup_inputs(seed: int = 0) -> dict:
    arg_keys = jax.random.split(jax.random.key(seed), 5)
    return {
        "grad": draw_grad(jax.random.fold_in(arg_keys[4], 71), 0),
        "owner": draw_owner(jax.random.fold_in(arg_keys[4], 71), 0),
        "left_root": draw_left_root(jax.random.fold_in(arg_keys[4], 71), 0),
        "right_root": draw_right_root(jax.random.fold_in(arg_keys[4], 71), 0),
    }


EPSILON = 1e-06

def precondition(block, left_factor, right_factor):
    left_part = jnp.dot(left_factor, block, preferred_element_type=jnp.float32).astype(jnp.bfloat16)
    product = jnp.dot(left_part, right_factor, preferred_element_type=jnp.float32)
    grad_mean = jnp.mean(jnp.square(block.astype(jnp.float32)))
    prod_mean = jnp.mean(jnp.square(product))
    update = product * (jnp.sqrt(grad_mean + EPSILON) / jnp.sqrt(prod_mean + EPSILON))
    return (update, jnp.sum(update * update))

def slot_numbers(owners_here, dp_size):
    onehot = (owners_here[..., None] == jnp.arange(dp_size, dtype=jnp.int32)).astype(jnp.int32)
    before = jnp.cumsum(onehot, axis=-2) - onehot
    return lax.optimization_barrier(jnp.sum(before * onehot, axis=-1)).astype(jnp.int32)

def reference(grad, owner, left_root, right_root):
    per_group = NBR * CB
    owners_here = owner.reshape(NBR, N_TENSOR, CB).transpose(1, 0, 2).reshape(N_TENSOR, per_group)
    slot_of = slot_numbers(owners_here, N_DP)
    position = (owners_here * SLOTS + slot_of).reshape(-1).astype(jnp.int32)
    tensor_of = jnp.repeat(jnp.arange(N_TENSOR, dtype=jnp.int32), per_group)
    blocks = grad.reshape(NBR, BLK, N_TENSOR, CB, BLK).transpose(2, 0, 3, 1, 4).reshape(N_TENSOR * per_group, BLK, BLK)

    def one_block(item):
        block, tensor_index, where = item
        return precondition(block, left_root[tensor_index, where], right_root[tensor_index, where])
    updates, squares = lax.map(one_block, (blocks, tensor_of, position))
    total_squares = jnp.sum(squares)
    update_rms = jnp.sqrt(total_squares / (ROWS * COLS) + EPSILON)
    inv_rms = 1.0 / update_rms
    direction = (updates * inv_rms).astype(jnp.bfloat16)
    direction = direction.reshape(N_TENSOR, NBR, CB, BLK, BLK).transpose(1, 3, 0, 2, 4).reshape(NBR, BLK, COLS)
    return (direction, update_rms)
```

```python
import functools

import jax
import jax.numpy as jnp
from jax import lax
from jax.experimental import pallas as pl
from jax.experimental.pallas import tpu as pltpu
from jax.sharding import PartitionSpec as P

BLK = 512
EPSILON = 1e-06
MESH = pl.DeviceIdType.MESH

NX = 4
SLOTS = 3
CELLS = NX * SLOTS
CHUNKS = 2
CAPACITY = (43, 38, 35, 29, 25, 20, 13, 8)


def block_cells(owners):
    n = owners.shape[-1]
    index = jnp.arange(n, dtype=jnp.int32)
    same = owners[:, :, None] == owners[:, None, :]
    slot = jnp.sum((same & (index[None, :] < index[:, None])).astype(jnp.int32), axis=-1)
    cell = owners * SLOTS + slot
    rank = jnp.sum((cell[:, None, :] < cell[:, :, None]).astype(jnp.int32), axis=-1)
    return cell, rank


def plane_split(cell, planes, capacity):
    n = cell.shape[-1]
    hops = len(capacity)
    planes_of = cell // CELLS
    z = jnp.arange(planes, dtype=jnp.int32)
    distance = (planes_of[:, None, :] - z[None, :, None]) % planes
    steps = jnp.arange(planes + 1, dtype=jnp.int32)
    nearer = jnp.sum((distance[:, :, None, :] < steps[None, None, :, None]).astype(jnp.int32), axis=-1)
    room = jnp.array(tuple(capacity) + (0,), jnp.int32)
    up_limit = jnp.min(nearer[:, :, 1 : hops + 2] + room, axis=-1)
    down_limit = jnp.max(nearer[:, :, planes - hops : planes + 1][:, :, ::-1] - room, axis=-1)
    local = nearer[:, :, 1]
    fits = jnp.all(down_limit <= up_limit)
    cut = jnp.clip((down_limit + up_limit) // 2, local, n)
    starts = jnp.sum((planes_of[:, None, :] < z[None, :, None]).astype(jnp.int32), axis=-1)
    return starts + cut, cut - local, fits


def make_table(cell, rank, ends, ups, devices):
    n = cell.shape[0]
    index = jnp.arange(n, dtype=jnp.int32)
    hit = (rank[None, :] == index[:, None]).astype(jnp.int32)
    block_of = jnp.sum(hit * index[None, :], axis=-1)
    cell_of = jnp.sum(hit * cell[None, :], axis=-1)
    cells = jnp.arange(devices * SLOTS, dtype=jnp.int32)
    below = jnp.sum((cell[None, :] < cells[:, None]).astype(jnp.int32), axis=-1)
    return jnp.concatenate([block_of, cell_of, rank, below, ends, ups])


def fold(piece):
    return jnp.concatenate([piece[:, :128], piece[:, 128:]], axis=0).astype(jnp.bfloat16)


def loop(count, body, unroll):
    turns = count // unroll

    def turn(t, carry):
        for u in range(unroll):
            body(t * unroll + u)
        return carry

    if turns:
        lax.fori_loop(0, turns, turn, 0)
    for j in range(turns * unroll, count):
        body(j)


def kernel(planes, nblk, capacity, *refs):
    hops = len(capacity)
    names = iter(refs)

    def take(*shape):
        if not shape:
            return next(names)
        return [take(*shape[1:]) for _ in range(shape[0])]

    tab, grad, left_hbm, right_hbm = take(4)
    out, ssq_out = take(2)
    left, right, mats, halves, prods, scales, squares = take(7)
    folded = take(CHUNKS)
    first = take(2, CHUNKS)
    ring = take(hops - 1, 2, CHUNKS)
    ring_last = take(CHUNKS)
    xs, xr, ys = take(3)
    back_send = take(hops, 2, CHUNKS)
    back = take(hops - 1, 2, CHUNKS)
    back_first = take(CHUNKS)
    back_last = take(CHUNKS)
    load_sem, ring_ss, ring_rs, x_ss, x_rs, y_ss, y_rs, back_ss, back_rs = take(9)

    rows = mats.shape[1]
    dp = lax.axis_index("dp")
    tensor = lax.axis_index("tensor")
    z, x = dp // NX, dp % NX
    devices = planes * NX
    per_row = nblk // grad.shape[0]
    CELL_OF, RANK_OF, BELOW = nblk, 2 * nblk, 3 * nblk
    ENDS = BELOW + devices * SLOTS
    UPS = ENDS + planes

    def plane(delta):
        return (z + (delta + planes)) % planes

    def device(zz, xx):
        return (zz * NX + xx, tensor)

    toward = [device(plane(1), x), device(plane(-1), x)]
    along = [None] + [device(z, (x + rel) % NX) for rel in range(1, NX)]

    factors = [
        pltpu.make_async_copy(left_hbm.at[0], left, load_sem.at[0]),
        pltpu.make_async_copy(right_hbm.at[0], right, load_sem.at[1]),
    ]
    for copy in factors:
        copy.start()

    barrier = pltpu.get_barrier_semaphore()
    peers = toward + along[1:]
    for peer in peers:
        pl.semaphore_signal(barrier, inc=1, device_id=peer, device_id_type=MESH)

    def fold_row(r):
        for c in range(per_row):
            piece = grad[r, :, pl.ds(c * BLK, BLK)].astype(jnp.float32)
            for h in range(CHUNKS):
                folded[h][r * per_row + c] = fold(piece[:, h * 256 : (h + 1) * 256])

    loop(grad.shape[0], fold_row, 2)

    end = tab[ENDS + z]

    def fill_first(j):
        for d, r in ((0, (end - 1 - j) & (nblk - 1)), (1, (end + j) & (nblk - 1))):
            block = tab[r]
            for h in range(CHUNKS):
                first[d][h][j] = folded[h][block]

    loop(capacity[0], fill_first, 4)

    pl.semaphore_wait(barrier, len(peers))

    sends = []

    def remote(src, dst, ss, rs, target):
        copy = pltpu.make_async_remote_copy(
            src_ref=src, dst_ref=dst, send_sem=ss, recv_sem=rs, device_id=target, device_id_type=MESH
        )
        copy.start()
        sends.append(copy)
        return copy

    ring_copies = {}

    def ring_at(k, d, h):
        if k < hops:
            return ring[k - 1][d][h]
        return ring_last[h].at[pl.ds(d * capacity[k - 1], capacity[k - 1])]

    def send_ring(k, d, h):
        src = first[d][h] if k == 1 else ring_at(k - 1, d, h).at[pl.ds(0, capacity[k - 1])]
        ring_copies[k, d, h] = remote(
            src, ring_at(k, d, h), ring_ss.at[k - 1, d, h], ring_rs.at[k - 1, d, h], toward[d]
        )

    for h in range(CHUNKS):
        for d in range(2):
            send_ring(1, d, h)

    x_copies = {}

    def send_x(delta, h):
        x_copies[delta, h] = [
            remote(xs.at[delta, h, rel], xr.at[delta, h, rel], x_ss.at[delta, h, rel], x_rs.at[delta, h, rel], along[rel])
            for rel in range(1, NX)
        ]

    def put_x(delta, h, rel, s, value):
        if rel == 0:
            xr[delta, h, 0, s] = value
        else:
            xs[delta, h, rel, s] = value

    def cell_index(rel, s):
        return z * CELLS + ((x + rel) % NX) * SLOTS + s

    for rel in range(NX):
        for s in range(SLOTS):
            rank = tab[BELOW + cell_index(rel, s)]
            block = tab[jnp.minimum(rank, nblk - 1)]
            for h in range(CHUNKS):
                put_x(0, h, rel, s, folded[h][block])
    for h in range(CHUNKS):
        send_x(0, h)

    def pick(delta, h):
        source = plane(-delta)
        source_end, source_ups = tab[ENDS + source], tab[UPS + source]
        k = min(delta, planes - delta)
        room = capacity[k - 1]
        for rel in range(NX):
            for s in range(SLOTS):
                rank = tab[BELOW + cell_index(rel, s)]
                up = (source_end - 1 - rank) & (nblk - 1)
                down = (rank - source_end) & (nblk - 1)
                if k == hops:
                    at = jnp.where(up < source_ups, jnp.minimum(up, room - 1), room + jnp.minimum(down, room - 1))
                    value = ring_last[h][at]
                elif delta < hops:
                    value = ring[k - 1][0][h][jnp.minimum(up, room - 1)]
                else:
                    value = ring[k - 1][1][h][jnp.minimum(down, room - 1)]
                put_x(delta, h, rel, s, value)
        send_x(delta, h)

    squares[...] = jnp.zeros_like(squares)

    def place(delta, h):
        for copy in x_copies[delta, h]:
            copy.wait_recv()
        source = plane(-delta)
        for s in range(SLOTS):
            total = None
            for pair in range(NX // 2):
                low, high = (
                    xr[delta, h, (x - (2 * pair + i) + NX) % NX, s].astype(jnp.float32) for i in range(2)
                )
                term = low * low + high * high
                total = term if total is None else total + term
                at = pl.ds(pl.multiple_of(source * (8 * NX) + 16 * pair, 16), 16)
                mats[s, at, pl.ds(h * 256, 128)] = jnp.concatenate([low[:8], high[:8]], 0).astype(jnp.bfloat16)
                mats[s, at, pl.ds(h * 256 + 128, 128)] = jnp.concatenate([low[8:], high[8:]], 0).astype(jnp.bfloat16)
            squares[s] += total

    pending = [(0, h) for h in range(CHUNKS)]
    for k in range(1, hops + 1):
        for h in range(CHUNKS):
            for d in range(2):
                ring_copies[k, d, h].wait_recv()
                if k < hops:
                    send_ring(k + 1, d, h)
            ready = []
            for delta in sorted({k, planes - k}):
                ready.append((delta, h))
            for delta, hh in ready:
                pick(delta, hh)
            while len(pending) > 4:
                place(*pending.pop(0))
            pending += ready
    for copy in factors:
        copy.wait()
    for h in range(CHUNKS):
        for item in [p for p in pending if p[1] == h]:
            place(*item)

        def left_part(s, carry):
            part = jnp.dot(left[s], mats[s, :, pl.ds(h * 256, 256)], preferred_element_type=jnp.float32)
            halves[s, :, pl.ds(h * 256, 256)] = part.astype(jnp.bfloat16)
            return carry

        lax.fori_loop(0, SLOTS, left_part, 0)

    cells = rows * BLK

    def right_part(s, total):
        product = jnp.dot(halves[s], right[s], preferred_element_type=jnp.float32)
        prods[s] = product
        prod_sum = jnp.sum(product * product, keepdims=True)
        grad_sum = jnp.sum(squares[s], keepdims=True)
        scale = jnp.sqrt(grad_sum / cells + EPSILON) / jnp.sqrt(prod_sum / cells + EPSILON)
        scales[s] = jnp.broadcast_to(scale, (8, 128))
        own = tab[BELOW + dp * SLOTS + s]
        found = jnp.full((1, 1), tab[CELL_OF + jnp.minimum(own, nblk - 1)])
        held = found == jnp.full((1, 1), dp * SLOTS + s)
        return total + jnp.where(held, prod_sum * scale * scale, 0.0)

    total = lax.fori_loop(0, SLOTS, right_part, jnp.zeros((1, 1), jnp.float32))
    ssq_out[...] = jnp.broadcast_to(total, ssq_out.shape)

    y_copies = {}

    def y_at(delta, h):
        if delta == 0:
            return back_last[h], 2 * capacity[0]
        if delta == hops:
            return back_first[h], 0
        k, d = (delta, 1) if delta < hops else (planes - delta, 0)
        return back[k - 1][d][h], capacity[k]

    def send_y(delta):
        target = plane(delta)
        for s in range(SLOTS):
            scale = scales[s][:, :1]
            for rel in range(NX):
                xx = (x + rel) % NX
                value = prods[s, pl.ds(pl.multiple_of((target * NX + xx) * 8, 8), 8), :] * scale
                for h in range(CHUNKS):
                    part = fold(value[:, h * 256 : (h + 1) * 256])
                    if rel == 0:
                        ref, row = y_at(delta, h)
                        ref[row + x * SLOTS + s] = part
                    else:
                        ys[delta, h, rel, s] = part
        for h in range(CHUNKS):
            ref, row = y_at(delta, h)
            y_copies[delta, h] = [
                remote(
                    ys.at[delta, h, rel], ref.at[pl.ds(row + x * SLOTS, SLOTS)],
                    y_ss.at[delta, h, rel], y_rs.at[delta, h, rel], along[rel],
                )
                for rel in range(1, NX)
            ]

    def wait_y(delta, h):
        for copy in y_copies.pop((delta, h), ()):
            copy.wait_recv()

    back_copies = {}

    def send_back(k, d, h):
        if k < hops:
            back_copies[k + 1, d, h].wait_recv()
        delta = planes - k if d == 0 else k
        wait_y(delta, h)
        target_end = tab[ENDS + plane(delta)]
        low = z * CELLS
        width = capacity[k - 1]
        filled = capacity[k] if k < hops else 0

        ref, row = y_at(delta, h)

        def merge(j, keep):
            rank = (target_end - 1 - j if d == 0 else target_end + j) & (nblk - 1)
            local = tab[CELL_OF + rank] - low
            at = row + jnp.clip(local, 0, CELLS - 1)
            if keep:
                at = jnp.where((local >= 0) & (local < CELLS), at, j)
            back_send[k - 1][d][h][j] = ref[at]

        loop(filled, functools.partial(merge, keep=True), 8)
        loop(width - filled, lambda j: merge(filled + j, False), 8)
        if k > 1:
            landing = back[k - 2][d][h].at[pl.ds(0, width)]
        else:
            landing = back_last[h].at[pl.ds(d * width, width)]
        back_copies[k, d, h] = remote(
            back_send[k - 1][d][h], landing,
            back_ss.at[k - 1, d, h], back_rs.at[k - 1, d, h], toward[1 - d],
        )

    sent = set()

    def ensure_y(delta):
        if delta not in sent:
            sent.add(delta)
            send_y(delta)

    for k in range(hops, 0, -1):
        for d in range(2):
            ensure_y(planes - k if d == 0 else k)
        for delta in (planes - k + 1, k - 1):
            if k == hops and 0 < delta < planes:
                ensure_y(delta)
        for h in range(CHUNKS):
            for d in range(2):
                send_back(k, d, h)
    ensure_y(0)

    end = tab[ENDS + z]
    ups = tab[UPS + z]
    for h in range(CHUNKS):
        for d in range(2):
            back_copies[1, d, h].wait_recv()
        wait_y(0, h)

        def finish(b, h=h):
            rank = tab[RANK_OF + b]
            local = tab[CELL_OF + rank] - z * CELLS
            up = (end - 1 - rank) & (nblk - 1)
            down = (rank - end) & (nblk - 1)
            room = capacity[0]
            at = jnp.where(up < ups, jnp.minimum(up, room - 1), room + jnp.minimum(down, room - 1))
            mine = (local >= 0) & (local < CELLS)
            at = jnp.where(mine, 2 * room + jnp.clip(local, 0, CELLS - 1), at)
            value = back_last[h][at].astype(jnp.float32)
            wide = jnp.concatenate([value[:8], value[8:]], axis=1).astype(jnp.bfloat16)
            column = (b % per_row) * BLK + h * 256
            out[b // per_row, :, pl.ds(pl.multiple_of(column, 256), 256)] = wide

        loop(nblk, finish, 8)

    for copy in sends:
        copy.wait_send()


def ring_call(grad, table, left_root, right_root, planes, capacity):
    row_blocks, piece_rows, width = grad.shape
    nblk = row_blocks * (width // BLK)
    rows = left_root.shape[-1]
    hops = len(capacity)
    tile = (16, 128)
    bf16, f32 = jnp.bfloat16, jnp.float32
    vmem = pltpu.VMEM
    dma = pltpu.SemaphoreType.DMA

    def tiles(*counts):
        return [vmem((count, *tile), bf16) for count in counts for _ in range(CHUNKS)]

    scratch = [
        vmem((SLOTS, rows, rows), bf16),
        vmem((SLOTS, BLK, BLK), bf16),
        vmem((SLOTS, rows, BLK), bf16),
        vmem((SLOTS, rows, BLK), bf16),
        vmem((SLOTS, rows, BLK), f32),
        vmem((SLOTS, 8, 128), f32),
        vmem((SLOTS, *tile), f32),
    ]
    twice = [capacity[k // 2] for k in range(2 * hops)]
    scratch += tiles(nblk)
    scratch += tiles(*twice[:2])
    scratch += tiles(*twice[:-2])
    scratch += tiles(2 * capacity[-1])
    scratch += [vmem((planes, CHUNKS, NX, SLOTS, *tile), bf16) for _ in range(3)]
    scratch += tiles(*twice)
    scratch += tiles(*[count + CELLS for count in twice[2:]])
    scratch += tiles(CELLS)
    scratch += tiles(2 * capacity[0] + CELLS)
    scratch += [dma((2,))]
    scratch += [dma((hops, 2, CHUNKS))] * 2
    scratch += [dma((planes, CHUNKS, NX))] * 4
    scratch += [dma((hops, 2, CHUNKS))] * 2
    body = functools.partial(kernel, planes, nblk, capacity)
    in_vmem = pl.BlockSpec(memory_space=pltpu.VMEM)
    return pl.pallas_call(
        body,
        out_shape=(
            jax.ShapeDtypeStruct(grad.shape, bf16),
            jax.ShapeDtypeStruct((8, 128), f32),
        ),
        in_specs=[
            pl.BlockSpec(memory_space=pltpu.SMEM),
            in_vmem,
            pl.BlockSpec(memory_space=pl.ANY),
            pl.BlockSpec(memory_space=pl.ANY),
        ],
        out_specs=(in_vmem, in_vmem),
        scratch_shapes=scratch,
        compiler_params=pltpu.CompilerParams(
            collective_id=0, has_side_effects=True, vmem_limit_bytes=50 * 1024 * 1024
        ),
        cost_estimate=pl.CostEstimate(
            flops=4 * SLOTS * rows * rows * BLK, bytes_accessed=4 * 1024 * 1024, transcendentals=0
        ),
        name="sorted_ring",
    )(table, grad, left_root, right_root)


def precondition(block, left_factor, right_factor):
    left_part = jnp.dot(left_factor, block, preferred_element_type=jnp.float32).astype(jnp.bfloat16)
    product = jnp.dot(left_part, right_factor, preferred_element_type=jnp.float32)
    grad_mean = jnp.mean(jnp.square(block.astype(jnp.float32)))
    prod_mean = jnp.mean(jnp.square(product))
    update = product * (jnp.sqrt(grad_mean + EPSILON) / jnp.sqrt(prod_mean + EPSILON))
    return (update, jnp.sum(update * update))


def padded_call(grad, cell, left_root, right_root, dp_size):
    row_blocks, piece_rows, width = grad.shape
    col_blocks = width // BLK
    per_group = row_blocks * col_blocks
    position = (cell % SLOTS) * dp_size + cell // SLOTS
    select = (position[None, :] == jnp.arange(SLOTS * dp_size, dtype=jnp.int32)[:, None]).astype(jnp.bfloat16)
    pieces = (
        grad.reshape(row_blocks, piece_rows, col_blocks, BLK)
        .transpose(0, 2, 1, 3)
        .reshape(per_group, piece_rows * BLK)
    )
    outgoing = jnp.dot(select, pieces, preferred_element_type=jnp.float32).astype(jnp.bfloat16)
    outgoing = outgoing.reshape(SLOTS, dp_size * piece_rows, BLK)
    arrived = lax.all_to_all(outgoing, "dp", split_axis=1, concat_axis=1, tiled=True)
    outcomes = [precondition(arrived[s], left_root[0, s], right_root[0, s]) for s in range(SLOTS)]
    updates = jnp.stack([outcome[0] for outcome in outcomes]).astype(jnp.bfloat16)
    partial_sum = sum([outcome[1] for outcome in outcomes])
    returned = lax.all_to_all(updates, "dp", split_axis=1, concat_axis=1, tiled=True)
    placed = jnp.take(returned.reshape(SLOTS * dp_size, piece_rows * BLK), position, axis=0)
    placed = placed.reshape(row_blocks, col_blocks, piece_rows, BLK).transpose(0, 2, 1, 3)
    return placed.reshape(row_blocks, piece_rows, width), partial_sum


def per_device(capacity, grad, owner, left_root, right_root):
    row_blocks, piece_rows, width = grad.shape
    dp_size = lax.axis_size("dp")
    tensors = lax.axis_size("tensor")
    planes = dp_size // NX
    col_blocks = width // BLK
    owners = owner.reshape(row_blocks, tensors, col_blocks).transpose(1, 0, 2).reshape(tensors, -1)
    cell, rank = block_cells(owners)
    ends, ups, fits = plane_split(cell, planes, capacity)
    tables = jax.vmap(functools.partial(make_table, devices=dp_size))(cell, rank, ends, ups)
    tensor_index = lax.axis_index("tensor")
    table = lax.dynamic_index_in_dim(tables, tensor_index, 0, keepdims=False)
    cell_here = lax.dynamic_index_in_dim(cell, tensor_index, 0, keepdims=False)

    def fast(grad, table, cell_here, left_root, right_root):
        moved, squares = ring_call(grad, table, left_root, right_root, planes, capacity)
        return moved, squares[0, 0]

    def padded(grad, table, cell_here, left_root, right_root):
        return padded_call(grad, cell_here, left_root, right_root, dp_size)

    moved, squares = lax.cond(fits, fast, padded, grad, table, cell_here, left_root, right_root)
    squares = lax.psum(squares, ("dp", "tensor"))
    cells = row_blocks * piece_rows * dp_size * width * tensors
    update_rms = jnp.sqrt(squares / cells + EPSILON)
    direction = (moved.astype(jnp.float32) * (1.0 / update_rms)).astype(jnp.bfloat16)
    return (direction, update_rms)


def build(mesh, capacity):
    return jax.shard_map(
        functools.partial(per_device, capacity),
        mesh=mesh,
        in_specs=(
            P(None, "dp", "tensor"),
            P(),
            P("tensor", "dp", None, None),
            P("tensor", "dp", None, None),
        ),
        out_specs=(P(None, "dp", "tensor"), P()),
        check_vma=False,
    )


def solution(mesh):
    return build(mesh, CAPACITY)
```

```python
import functools

import jax
import jax.numpy as jnp
from jax import lax
from jax.experimental import pallas as pl
from jax.experimental.pallas import tpu as pltpu
from jax.sharding import PartitionSpec as P

BLK = 512
EPSILON = 1e-06
MESH = pl.DeviceIdType.MESH

NX = 4
SLOTS = 3
CELLS = NX * SLOTS
CHUNKS = 2
CAPACITY = (43, 38, 35, 29, 25, 20, 13, 8)


def block_cells(owners):
    n = owners.shape[-1]
    index = jnp.arange(n, dtype=jnp.int32)
    same = owners[:, :, None] == owners[:, None, :]
    slot = jnp.sum((same & (index[None, :] < index[:, None])).astype(jnp.int32), axis=-1)
    cell = owners * SLOTS + slot
    rank = jnp.sum((cell[:, None, :] < cell[:, :, None]).astype(jnp.int32), axis=-1)
    return cell, rank


def plane_split(cell, planes, capacity):
    n = cell.shape[-1]
    hops = len(capacity)
    planes_of = cell // CELLS
    z = jnp.arange(planes, dtype=jnp.int32)
    distance = (planes_of[:, None, :] - z[None, :, None]) % planes
    steps = jnp.arange(planes + 1, dtype=jnp.int32)
    nearer = jnp.sum((distance[:, :, None, :] < steps[None, None, :, None]).astype(jnp.int32), axis=-1)
    room = jnp.array(tuple(capacity) + (0,), jnp.int32)
    up_limit = jnp.min(nearer[:, :, 1 : hops + 2] + room, axis=-1)
    down_limit = jnp.max(nearer[:, :, planes - hops : planes + 1][:, :, ::-1] - room, axis=-1)
    local = nearer[:, :, 1]
    fits = jnp.all(down_limit <= up_limit)
    cut = jnp.clip((down_limit + up_limit) // 2, local, n)
    starts = jnp.sum((planes_of[:, None, :] < z[None, :, None]).astype(jnp.int32), axis=-1)
    return starts + cut, cut - local, fits


def make_table(cell, rank, ends, ups, devices):
    n = cell.shape[0]
    index = jnp.arange(n, dtype=jnp.int32)
    hit = (rank[None, :] == index[:, None]).astype(jnp.int32)
    block_of = jnp.sum(hit * index[None, :], axis=-1)
    cell_of = jnp.sum(hit * cell[None, :], axis=-1)
    cells = jnp.arange(devices * SLOTS, dtype=jnp.int32)
    below = jnp.sum((cell[None, :] < cells[:, None]).astype(jnp.int32), axis=-1)
    return jnp.concatenate([block_of, cell_of, rank, below, ends, ups])


def fold(piece):
    return jnp.concatenate([piece[:, :128], piece[:, 128:]], axis=0).astype(jnp.bfloat16)


def loop(count, body, unroll):
    turns = count // unroll

    def turn(t, carry):
        for u in range(unroll):
            body(t * unroll + u)
        return carry

    if turns:
        lax.fori_loop(0, turns, turn, 0)
    for j in range(turns * unroll, count):
        body(j)


def kernel(planes, nblk, capacity, *refs):
    hops = len(capacity)
    names = iter(refs)

    def take(*shape):
        if not shape:
            return next(names)
        return [take(*shape[1:]) for _ in range(shape[0])]

    tab, grad, left_hbm, right_hbm = take(4)
    out, rms_out = take(2)
    left, right, mats, halves, prods, scales, squares = take(7)
    folded = take(CHUNKS)
    first = take(2, CHUNKS)
    ring = take(hops - 1, 2, CHUNKS)
    ring_last = take(CHUNKS)
    xs, xr, ys = take(3)
    back_send = take(hops, 2, CHUNKS)
    back = take(hops - 1, 2, CHUNKS)
    back_first = take(CHUNKS)
    back_last = take(CHUNKS)
    sums = take()
    load_sem, ring_ss, ring_rs, x_ss, x_rs, y_ss, y_rs, back_ss, back_rs, sum_ss, sum_rs = take(11)

    rows = mats.shape[1]
    dp = lax.axis_index("dp")
    tensor = lax.axis_index("tensor")
    tensors = lax.axis_size("tensor")
    z, x = dp // NX, dp % NX
    devices = planes * NX
    per_row = nblk // grad.shape[0]
    CELL_OF, RANK_OF, BELOW = nblk, 2 * nblk, 3 * nblk
    ENDS = BELOW + devices * SLOTS
    UPS = ENDS + planes

    def plane(delta):
        return (z + (delta + planes)) % planes

    def device(zz, xx):
        return (zz * NX + xx, tensor)

    toward = [device(plane(1), x), device(plane(-1), x)]
    along = [None] + [device(z, (x + rel) % NX) for rel in range(1, NX)]

    factors = [
        pltpu.make_async_copy(left_hbm.at[0], left, load_sem.at[0]),
        pltpu.make_async_copy(right_hbm.at[0], right, load_sem.at[1]),
    ]
    for copy in factors:
        copy.start()

    barrier = pltpu.get_barrier_semaphore()
    partners = []
    stride = 1
    while stride < tensors:
        partners.append((dp, tensor + stride - 2 * stride * ((tensor // stride) % 2)))
        stride *= 2
    stride = 1
    while stride < devices:
        partners.append((dp + stride - 2 * stride * ((dp // stride) % 2), tensor))
        stride *= 2
    peers = toward + along[1:] + partners
    for peer in peers:
        pl.semaphore_signal(barrier, inc=1, device_id=peer, device_id_type=MESH)

    def fold_row(r):
        for c in range(per_row):
            piece = grad[r, :, pl.ds(c * BLK, BLK)].astype(jnp.float32)
            for h in range(CHUNKS):
                folded[h][r * per_row + c] = fold(piece[:, h * 256 : (h + 1) * 256])

    loop(grad.shape[0], fold_row, 2)

    end = tab[ENDS + z]

    def fill_first(j):
        for d, r in ((0, (end - 1 - j) & (nblk - 1)), (1, (end + j) & (nblk - 1))):
            block = tab[r]
            for h in range(CHUNKS):
                first[d][h][j] = folded[h][block]

    loop(capacity[0], fill_first, 4)

    pl.semaphore_wait(barrier, len(peers))

    sends = []

    def remote(src, dst, ss, rs, target):
        copy = pltpu.make_async_remote_copy(
            src_ref=src, dst_ref=dst, send_sem=ss, recv_sem=rs, device_id=target, device_id_type=MESH
        )
        copy.start()
        sends.append(copy)
        return copy

    ring_copies = {}

    def ring_at(k, d, h):
        if k < hops:
            return ring[k - 1][d][h]
        return ring_last[h].at[pl.ds(d * capacity[k - 1], capacity[k - 1])]

    def send_ring(k, d, h):
        src = first[d][h] if k == 1 else ring_at(k - 1, d, h).at[pl.ds(0, capacity[k - 1])]
        ring_copies[k, d, h] = remote(
            src, ring_at(k, d, h), ring_ss.at[k - 1, d, h], ring_rs.at[k - 1, d, h], toward[d]
        )

    for h in range(CHUNKS):
        for d in range(2):
            send_ring(1, d, h)

    x_copies = {}

    def send_x(delta, h):
        x_copies[delta, h] = [
            remote(xs.at[delta, h, rel], xr.at[delta, h, rel], x_ss.at[delta, h, rel], x_rs.at[delta, h, rel], along[rel])
            for rel in range(1, NX)
        ]

    def put_x(delta, h, rel, s, value):
        if rel == 0:
            xr[delta, h, 0, s] = value
        else:
            xs[delta, h, rel, s] = value

    def cell_index(rel, s):
        return z * CELLS + ((x + rel) % NX) * SLOTS + s

    for rel in range(NX):
        for s in range(SLOTS):
            rank = tab[BELOW + cell_index(rel, s)]
            block = tab[jnp.minimum(rank, nblk - 1)]
            for h in range(CHUNKS):
                put_x(0, h, rel, s, folded[h][block])
    for h in range(CHUNKS):
        send_x(0, h)

    def pick(delta, h):
        source = plane(-delta)
        source_end, source_ups = tab[ENDS + source], tab[UPS + source]
        k = min(delta, planes - delta)
        room = capacity[k - 1]
        for rel in range(NX):
            for s in range(SLOTS):
                rank = tab[BELOW + cell_index(rel, s)]
                up = (source_end - 1 - rank) & (nblk - 1)
                down = (rank - source_end) & (nblk - 1)
                if k == hops:
                    at = jnp.where(up < source_ups, jnp.minimum(up, room - 1), room + jnp.minimum(down, room - 1))
                    value = ring_last[h][at]
                elif delta < hops:
                    value = ring[k - 1][0][h][jnp.minimum(up, room - 1)]
                else:
                    value = ring[k - 1][1][h][jnp.minimum(down, room - 1)]
                put_x(delta, h, rel, s, value)
        send_x(delta, h)

    squares[...] = jnp.zeros_like(squares)

    def place(delta, h):
        for copy in x_copies[delta, h]:
            copy.wait_recv()
        source = plane(-delta)
        for s in range(SLOTS):
            total = None
            for pair in range(NX // 2):
                low, high = (
                    xr[delta, h, (x - (2 * pair + i) + NX) % NX, s].astype(jnp.float32) for i in range(2)
                )
                term = low * low + high * high
                total = term if total is None else total + term
                at = pl.ds(pl.multiple_of(source * (8 * NX) + 16 * pair, 16), 16)
                mats[s, at, pl.ds(h * 256, 128)] = jnp.concatenate([low[:8], high[:8]], 0).astype(jnp.bfloat16)
                mats[s, at, pl.ds(h * 256 + 128, 128)] = jnp.concatenate([low[8:], high[8:]], 0).astype(jnp.bfloat16)
            squares[s] += total

    pending = [(0, h) for h in range(CHUNKS)]
    for k in range(1, hops + 1):
        for h in range(CHUNKS):
            for d in range(2):
                ring_copies[k, d, h].wait_recv()
                if k < hops:
                    send_ring(k + 1, d, h)
            ready = []
            for delta in sorted({k, planes - k}):
                ready.append((delta, h))
            for delta, hh in ready:
                pick(delta, hh)
            while len(pending) > 4:
                place(*pending.pop(0))
            pending += ready
    for copy in factors:
        copy.wait()
    for h in range(CHUNKS):
        for item in [p for p in pending if p[1] == h]:
            place(*item)

        def left_part(s, carry):
            part = jnp.dot(left[s], mats[s, :, pl.ds(h * 256, 256)], preferred_element_type=jnp.float32)
            halves[s, :, pl.ds(h * 256, 256)] = part.astype(jnp.bfloat16)
            return carry

        lax.fori_loop(0, SLOTS, left_part, 0)

    cells = rows * BLK

    def right_part(s, total):
        product = jnp.dot(halves[s], right[s], preferred_element_type=jnp.float32)
        prods[s] = product
        prod_sum = jnp.sum(product * product, keepdims=True)
        grad_sum = jnp.sum(squares[s], keepdims=True)
        scale = jnp.sqrt(grad_sum / cells + EPSILON) / jnp.sqrt(prod_sum / cells + EPSILON)
        scales[s] = jnp.broadcast_to(scale, (8, 128))
        own = tab[BELOW + dp * SLOTS + s]
        found = jnp.full((1, 1), tab[CELL_OF + jnp.minimum(own, nblk - 1)])
        held = found == jnp.full((1, 1), dp * SLOTS + s)
        return total + jnp.where(held, prod_sum * scale * scale, 0.0)

    total = lax.fori_loop(0, SLOTS, right_part, jnp.zeros((1, 1), jnp.float32))
    stages = len(partners)
    sums[0] = jnp.broadcast_to(total, sums.shape[1:])
    sum_copies = []

    def exchange():
        i = len(sum_copies)
        if i:
            sum_copies[i - 1].wait_recv()
            sums[2 * i] = sums[2 * i - 2] + sums[2 * i - 1]
        if i < stages:
            sum_copies.append(
                remote(sums.at[2 * i], sums.at[2 * i + 1], sum_ss.at[i], sum_rs.at[i], partners[i])
            )


    y_copies = {}

    def y_at(delta, h):
        if delta == 0:
            return back_last[h], 2 * capacity[0]
        if delta == hops:
            return back_first[h], 0
        k, d = (delta, 1) if delta < hops else (planes - delta, 0)
        return back[k - 1][d][h], capacity[k]

    def send_y(delta):
        target = plane(delta)
        for s in range(SLOTS):
            scale = scales[s][:, :1]
            for rel in range(NX):
                xx = (x + rel) % NX
                value = prods[s, pl.ds(pl.multiple_of((target * NX + xx) * 8, 8), 8), :] * scale
                for h in range(CHUNKS):
                    part = fold(value[:, h * 256 : (h + 1) * 256])
                    if rel == 0:
                        ref, row = y_at(delta, h)
                        ref[row + x * SLOTS + s] = part
                    else:
                        ys[delta, h, rel, s] = part
        for h in range(CHUNKS):
            ref, row = y_at(delta, h)
            y_copies[delta, h] = [
                remote(
                    ys.at[delta, h, rel], ref.at[pl.ds(row + x * SLOTS, SLOTS)],
                    y_ss.at[delta, h, rel], y_rs.at[delta, h, rel], along[rel],
                )
                for rel in range(1, NX)
            ]

    def wait_y(delta, h):
        for copy in y_copies.pop((delta, h), ()):
            copy.wait_recv()

    back_copies = {}

    def send_back(k, d, h):
        if k < hops:
            back_copies[k + 1, d, h].wait_recv()
        delta = planes - k if d == 0 else k
        wait_y(delta, h)
        target_end = tab[ENDS + plane(delta)]
        low = z * CELLS
        width = capacity[k - 1]
        filled = capacity[k] if k < hops else 0

        ref, row = y_at(delta, h)

        def merge(j, keep):
            rank = (target_end - 1 - j if d == 0 else target_end + j) & (nblk - 1)
            local = tab[CELL_OF + rank] - low
            at = row + jnp.clip(local, 0, CELLS - 1)
            if keep:
                at = jnp.where((local >= 0) & (local < CELLS), at, j)
            back_send[k - 1][d][h][j] = ref[at]

        loop(filled, functools.partial(merge, keep=True), 8)
        loop(width - filled, lambda j: merge(filled + j, False), 8)
        if k > 1:
            landing = back[k - 2][d][h].at[pl.ds(0, width)]
        else:
            landing = back_last[h].at[pl.ds(d * width, width)]
        back_copies[k, d, h] = remote(
            back_send[k - 1][d][h], landing,
            back_ss.at[k - 1, d, h], back_rs.at[k - 1, d, h], toward[1 - d],
        )

    sent = set()

    def ensure_y(delta):
        if delta not in sent:
            sent.add(delta)
            send_y(delta)

    for k in range(hops, 0, -1):
        for d in range(2):
            ensure_y(planes - k if d == 0 else k)
        for delta in (planes - k + 1, k - 1):
            if k == hops and 0 < delta < planes:
                ensure_y(delta)
        for h in range(CHUNKS):
            for d in range(2):
                send_back(k, d, h)
            if len(sum_copies) < stages:
                exchange()
    ensure_y(0)
    while len(sum_copies) < stages:
        exchange()
    exchange()
    update_rms = jnp.sqrt(sums[2 * stages] / (nblk * cells * tensors) + EPSILON)
    rms_out[...] = update_rms
    inv_rms = (1.0 / update_rms)[:1, :1]

    end = tab[ENDS + z]
    ups = tab[UPS + z]
    for h in range(CHUNKS):
        for d in range(2):
            back_copies[1, d, h].wait_recv()
        wait_y(0, h)

        def finish(b, h=h):
            rank = tab[RANK_OF + b]
            local = tab[CELL_OF + rank] - z * CELLS
            up = (end - 1 - rank) & (nblk - 1)
            down = (rank - end) & (nblk - 1)
            room = capacity[0]
            at = jnp.where(up < ups, jnp.minimum(up, room - 1), room + jnp.minimum(down, room - 1))
            mine = (local >= 0) & (local < CELLS)
            at = jnp.where(mine, 2 * room + jnp.clip(local, 0, CELLS - 1), at)
            value = back_last[h][at].astype(jnp.float32) * inv_rms
            wide = jnp.concatenate([value[:8], value[8:]], axis=1).astype(jnp.bfloat16)
            column = (b % per_row) * BLK + h * 256
            out[b // per_row, :, pl.ds(pl.multiple_of(column, 256), 256)] = wide

        loop(nblk, finish, 8)

    for copy in sends:
        copy.wait_send()


def ring_call(grad, table, left_root, right_root, planes, tensors, capacity):
    row_blocks, piece_rows, width = grad.shape
    nblk = row_blocks * (width // BLK)
    rows = left_root.shape[-1]
    hops = len(capacity)
    tile = (16, 128)
    bf16, f32 = jnp.bfloat16, jnp.float32
    vmem = pltpu.VMEM
    dma = pltpu.SemaphoreType.DMA

    def tiles(*counts):
        return [vmem((count, *tile), bf16) for count in counts for _ in range(CHUNKS)]

    scratch = [
        vmem((SLOTS, rows, rows), bf16),
        vmem((SLOTS, BLK, BLK), bf16),
        vmem((SLOTS, rows, BLK), bf16),
        vmem((SLOTS, rows, BLK), bf16),
        vmem((SLOTS, rows, BLK), f32),
        vmem((SLOTS, 8, 128), f32),
        vmem((SLOTS, *tile), f32),
    ]
    twice = [capacity[k // 2] for k in range(2 * hops)]
    scratch += tiles(nblk)
    scratch += tiles(*twice[:2])
    scratch += tiles(*twice[:-2])
    scratch += tiles(2 * capacity[-1])
    scratch += [vmem((planes, CHUNKS, NX, SLOTS, *tile), bf16) for _ in range(3)]
    scratch += tiles(*twice)
    scratch += tiles(*[count + CELLS for count in twice[2:]])
    scratch += tiles(CELLS)
    scratch += tiles(2 * capacity[0] + CELLS)
    stages = (planes * NX * tensors).bit_length() - 1
    scratch += [vmem((2 * stages + 1, 8, 128), f32)]
    scratch += [dma((2,))]
    scratch += [dma((hops, 2, CHUNKS))] * 2
    scratch += [dma((planes, CHUNKS, NX))] * 4
    scratch += [dma((hops, 2, CHUNKS))] * 2
    scratch += [dma((stages,))] * 2
    body = functools.partial(kernel, planes, nblk, capacity)
    in_vmem = pl.BlockSpec(memory_space=pltpu.VMEM)
    return pl.pallas_call(
        body,
        out_shape=(
            jax.ShapeDtypeStruct(grad.shape, bf16),
            jax.ShapeDtypeStruct((8, 128), f32),
        ),
        in_specs=[
            pl.BlockSpec(memory_space=pltpu.SMEM),
            in_vmem,
            pl.BlockSpec(memory_space=pl.ANY),
            pl.BlockSpec(memory_space=pl.ANY),
        ],
        out_specs=(in_vmem, in_vmem),
        scratch_shapes=scratch,
        compiler_params=pltpu.CompilerParams(
            collective_id=0, has_side_effects=True, vmem_limit_bytes=50 * 1024 * 1024
        ),
        cost_estimate=pl.CostEstimate(
            flops=4 * SLOTS * rows * rows * BLK, bytes_accessed=4 * 1024 * 1024, transcendentals=0
        ),
        name="sorted_ring",
    )(table, grad, left_root, right_root)


def precondition(block, left_factor, right_factor):
    left_part = jnp.dot(left_factor, block, preferred_element_type=jnp.float32).astype(jnp.bfloat16)
    product = jnp.dot(left_part, right_factor, preferred_element_type=jnp.float32)
    grad_mean = jnp.mean(jnp.square(block.astype(jnp.float32)))
    prod_mean = jnp.mean(jnp.square(product))
    update = product * (jnp.sqrt(grad_mean + EPSILON) / jnp.sqrt(prod_mean + EPSILON))
    return (update, jnp.sum(update * update))


def padded_call(grad, cell, left_root, right_root, dp_size):
    row_blocks, piece_rows, width = grad.shape
    col_blocks = width // BLK
    per_group = row_blocks * col_blocks
    position = (cell % SLOTS) * dp_size + cell // SLOTS
    select = (position[None, :] == jnp.arange(SLOTS * dp_size, dtype=jnp.int32)[:, None]).astype(jnp.bfloat16)
    pieces = (
        grad.reshape(row_blocks, piece_rows, col_blocks, BLK)
        .transpose(0, 2, 1, 3)
        .reshape(per_group, piece_rows * BLK)
    )
    outgoing = jnp.dot(select, pieces, preferred_element_type=jnp.float32).astype(jnp.bfloat16)
    outgoing = outgoing.reshape(SLOTS, dp_size * piece_rows, BLK)
    arrived = lax.all_to_all(outgoing, "dp", split_axis=1, concat_axis=1, tiled=True)
    outcomes = [precondition(arrived[s], left_root[0, s], right_root[0, s]) for s in range(SLOTS)]
    updates = jnp.stack([outcome[0] for outcome in outcomes]).astype(jnp.bfloat16)
    partial_sum = sum([outcome[1] for outcome in outcomes])
    returned = lax.all_to_all(updates, "dp", split_axis=1, concat_axis=1, tiled=True)
    placed = jnp.take(returned.reshape(SLOTS * dp_size, piece_rows * BLK), position, axis=0)
    placed = placed.reshape(row_blocks, col_blocks, piece_rows, BLK).transpose(0, 2, 1, 3)
    cells = per_group * dp_size * piece_rows * BLK * lax.axis_size("tensor")
    update_rms = jnp.sqrt(lax.psum(partial_sum, ("dp", "tensor")) / cells + EPSILON)
    direction = placed.reshape(row_blocks, piece_rows, width).astype(jnp.float32) * (1.0 / update_rms)
    return direction.astype(jnp.bfloat16), update_rms


def per_device(capacity, grad, owner, left_root, right_root):
    row_blocks, piece_rows, width = grad.shape
    dp_size = lax.axis_size("dp")
    tensors = lax.axis_size("tensor")
    planes = dp_size // NX
    col_blocks = width // BLK
    owners = owner.reshape(row_blocks, tensors, col_blocks).transpose(1, 0, 2).reshape(tensors, -1)
    cell, rank = block_cells(owners)
    ends, ups, fits = plane_split(cell, planes, capacity)
    tables = jax.vmap(functools.partial(make_table, devices=dp_size))(cell, rank, ends, ups)
    tensor_index = lax.axis_index("tensor")
    table = lax.dynamic_index_in_dim(tables, tensor_index, 0, keepdims=False)
    cell_here = lax.dynamic_index_in_dim(cell, tensor_index, 0, keepdims=False)

    def fast(grad, table, cell_here, left_root, right_root):
        moved, rms = ring_call(grad, table, left_root, right_root, planes, tensors, capacity)
        return moved, rms[0, 0]

    def padded(grad, table, cell_here, left_root, right_root):
        return padded_call(grad, cell_here, left_root, right_root, dp_size)

    return lax.cond(fits, fast, padded, grad, table, cell_here, left_root, right_root)


def build(mesh, capacity):
    return jax.shard_map(
        functools.partial(per_device, capacity),
        mesh=mesh,
        in_specs=(
            P(None, "dp", "tensor"),
            P(),
            P("tensor", "dp", None, None),
            P("tensor", "dp", None, None),
        ),
        out_specs=(P(None, "dp", "tensor"), P()),
        check_vma=False,
    )


def solution(mesh):
    return build(mesh, CAPACITY)
```

```python
import functools

import jax
import jax.numpy as jnp
from jax import lax
from jax.experimental import pallas as pl
from jax.experimental.pallas import tpu as pltpu
from jax.sharding import PartitionSpec as P

BLK = 512
EPSILON = 1e-06
MESH = pl.DeviceIdType.MESH

NX = 4
SLOTS = 3
CELLS = NX * SLOTS
CHUNKS = 2
BITS = (1, 2, 4, 8, 16, 32)
DISTANCE = ((0, 1, 2, 0, 0, 0), (1, 2, 1, 2, 4, 8))
CAPACITY = (42, 37, 34, 28, 24, 19, 12, 7)


def block_cells(owners):
    n = owners.shape[0]
    index = jnp.arange(n, dtype=jnp.int32)
    same = owners[:, None] == owners[None, :]
    slot = jnp.sum((same & (index[None, :] < index[:, None])).astype(jnp.int32), axis=1)
    cell = owners * SLOTS + slot
    rank = jnp.sum((cell[None, :] < cell[:, None]).astype(jnp.int32), axis=1)
    return cell, rank


def plane_split(owner, tensors, planes, capacity):
    hops = len(capacity)
    z = jnp.arange(planes, dtype=jnp.int32)
    counts = jnp.sum((owner[:, :, None] // NX == z).astype(jnp.float32), axis=0)
    counts = jnp.sum(counts.reshape(tensors, -1, planes), axis=1)
    q = jnp.arange(2 * planes + 1, dtype=jnp.int32)
    turns = (z[:, None] < q[None, :]).astype(jnp.float32) + (z[:, None] + planes < q[None, :]).astype(jnp.float32)
    below = jnp.dot(counts, turns, precision=lax.Precision.HIGHEST).astype(jnp.int32)
    room = tuple(capacity) + (0,)
    high, low = None, None
    for k in range(1, hops + 2):
        up = below[:, k : k + planes] + room[k - 1]
        down = below[:, planes + 1 - k : 2 * planes + 1 - k] - room[k - 1]
        high = up if high is None else jnp.minimum(high, up)
        low = down if low is None else jnp.maximum(low, down)
    first = below[:, 1 : planes + 1]
    ends = jnp.maximum((high + low) // 2, first)
    return ends, ends - first, jnp.all(low <= high)


def make_table(cell, rank, ends, ups, devices):
    n = cell.shape[0]
    index = jnp.arange(n, dtype=jnp.int32)
    hit = (rank[None, :] == index[:, None]).astype(jnp.int32)
    block_of = jnp.sum(hit * index[None, :], axis=-1)
    cell_of = jnp.sum(hit * cell[None, :], axis=-1)
    cells = jnp.arange(devices * SLOTS, dtype=jnp.int32)
    below = jnp.sum((cell[None, :] < cells[:, None]).astype(jnp.int32), axis=-1)
    return jnp.concatenate([block_of, cell_of, rank, below, ends, ups])


def fold(piece):
    return jnp.concatenate([piece[:, :128], piece[:, 128:]], axis=0).astype(jnp.bfloat16)


def loop(count, body, unroll):
    turns = count // unroll

    def turn(t, carry):
        for u in range(unroll):
            body(t * unroll + u)
        return carry

    if turns:
        lax.fori_loop(0, turns, turn, 0)
    for j in range(turns * unroll, count):
        body(j)


def kernel(planes, nblk, capacity, *refs):
    hops = len(capacity)
    names = iter(refs)

    def take(*shape):
        if not shape:
            return next(names)
        return [take(*shape[1:]) for _ in range(shape[0])]

    tab, grad, left_hbm, right_hbm = take(4)
    out, rms_out = take(2)
    left, right, mats, halves, prods, scales, squares = take(7)
    folded = take(CHUNKS)
    first = take(2, CHUNKS)
    ring = take(hops - 1, 2, CHUNKS)
    ring_last = take(CHUNKS)
    xs, xr, ys = take(3)
    back_send = take(hops, 2, CHUNKS)
    back = take(hops - 1, 2, CHUNKS)
    back_first = take(CHUNKS)
    back_last = take(CHUNKS)
    sums = take()
    load_sem, ring_ss, ring_rs, x_ss, x_rs, y_ss, y_rs, back_ss, back_rs, sum_ss, sum_rs = take(11)

    rows = mats.shape[1]
    dp = lax.axis_index("dp")
    tensor = lax.axis_index("tensor")
    tensors = lax.axis_size("tensor")
    z, x = dp // NX, dp % NX
    devices = planes * NX
    per_row = nblk // grad.shape[0]
    CELL_OF, RANK_OF, BELOW = nblk, 2 * nblk, 3 * nblk
    ENDS = BELOW + devices * SLOTS
    UPS = ENDS + planes

    def plane(delta):
        return (z + (delta + planes)) % planes

    def device(zz, xx):
        return (zz * NX + xx, tensor)

    toward = [device(plane(1), x), device(plane(-1), x)]
    along = [None] + [device(z, (x + rel) % NX) for rel in range(1, NX)]

    factors = [
        pltpu.make_async_copy(left_hbm.at[0], left, load_sem.at[0]),
        pltpu.make_async_copy(right_hbm.at[0], right, load_sem.at[1]),
    ]
    for copy in factors:
        copy.start()

    barrier = pltpu.get_barrier_semaphore()
    partners = []
    bits = [(stride, place) for place, size in ((0, tensors), (1, devices)) for stride in BITS if stride < size]
    for stride, place in sorted(bits, key=lambda bit: (DISTANCE[bit[1]][BITS.index(bit[0])], bit)):
        if place:
            partners.append((dp + stride - 2 * stride * ((dp // stride) % 2), tensor))
        else:
            partners.append((dp, tensor + stride - 2 * stride * ((tensor // stride) % 2)))
    peers = toward + along[1:] + [partner for partner in partners if partner[0] is dp]
    for peer in peers:
        pl.semaphore_signal(barrier, inc=1, device_id=peer, device_id_type=MESH)

    end = tab[ENDS + z]

    def fill_chunk(h):
        def fold_row(r):
            for c in range(per_row):
                piece = grad[r, :, pl.ds(c * BLK + h * 256, 256)].astype(jnp.float32)
                folded[h][r * per_row + c] = fold(piece)

        def fill_first(j):
            first[0][h][j] = folded[h][tab[(end - 1 - j) & (nblk - 1)]]
            first[1][h][j] = folded[h][tab[(end + j) & (nblk - 1)]]

        loop(grad.shape[0], fold_row, 4)
        loop(capacity[0], fill_first, 8)

    fill_chunk(0)
    pl.semaphore_wait(barrier, len(peers))

    sends = []

    def describe(src, dst, ss, rs, target):
        return pltpu.make_async_remote_copy(
            src_ref=src, dst_ref=dst, send_sem=ss, recv_sem=rs, device_id=target, device_id_type=MESH
        )

    def start(*args):
        copy = describe(*args)
        copy.start()
        return copy

    def remote(*args):
        copy = start(*args)
        sends.append(copy)
        return copy

    ring_copies = {}

    def ring_at(k, d, h):
        if k < hops:
            return ring[k - 1][d][h]
        return ring_last[h].at[pl.ds(d * capacity[k - 1], capacity[k - 1])]

    def send_ring(k, d, h):
        src = first[d][h] if k == 1 else ring_at(k - 1, d, h).at[pl.ds(0, capacity[k - 1])]
        ring_copies[k, d, h] = remote(
            src, ring_at(k, d, h), ring_ss.at[k - 1, d, h], ring_rs.at[k - 1, d, h], toward[d]
        )

    for h in range(CHUNKS):
        if h:
            fill_chunk(h)
        for d in range(2):
            send_ring(1, d, h)

    def send_x(delta, h):
        for rel in range(1, NX):
            start(xs.at[delta, h, rel - 1], xr.at[delta, h, rel], x_ss.at[0], x_rs.at[delta, h], along[rel])

    def put_x(delta, h, rel, s, value):
        if rel == 0:
            xr[delta, h, 0, s] = value
        else:
            xs[delta, h, rel - 1, s] = value

    def cell_index(rel, s):
        return z * CELLS + ((x + rel) % NX) * SLOTS + s

    for rel in range(NX):
        for s in range(SLOTS):
            rank = tab[BELOW + cell_index(rel, s)]
            block = tab[jnp.minimum(rank, nblk - 1)]
            for h in range(CHUNKS):
                put_x(0, h, rel, s, folded[h][block])
    for h in range(CHUNKS):
        send_x(0, h)

    def pick(delta, h):
        source = plane(-delta)
        source_end, source_ups = tab[ENDS + source], tab[UPS + source]
        k = min(delta, planes - delta)
        room = capacity[k - 1]
        for rel in range(NX):
            for s in range(SLOTS):
                rank = tab[BELOW + cell_index(rel, s)]
                up = (source_end - 1 - rank) & (nblk - 1)
                down = (rank - source_end) & (nblk - 1)
                if k == hops:
                    at = jnp.where(up < source_ups, jnp.minimum(up, room - 1), room + jnp.minimum(down, room - 1))
                    value = ring_last[h][at]
                elif delta < hops:
                    value = ring[k - 1][0][h][jnp.minimum(up, room - 1)]
                else:
                    value = ring[k - 1][1][h][jnp.minimum(down, room - 1)]
                put_x(delta, h, rel, s, value)
        send_x(delta, h)

    squares[...] = jnp.zeros_like(squares)

    def place(delta, h):
        arrived = xr.at[delta, h, pl.ds(1, NX - 1)]
        describe(arrived, arrived, x_ss.at[0], x_rs.at[delta, h], along[1]).wait_recv()
        source = plane(-delta)
        for s in range(SLOTS):
            total = None
            for pair in range(NX // 2):
                low, high = (
                    xr[delta, h, (x - (2 * pair + i) + NX) % NX, s].astype(jnp.float32) for i in range(2)
                )
                term = low * low + high * high
                total = term if total is None else total + term
                at = pl.ds(pl.multiple_of(source * (8 * NX) + 16 * pair, 16), 16)
                mats[s, at, pl.ds(h * 256, 128)] = jnp.concatenate([low[:8], high[:8]], 0).astype(jnp.bfloat16)
                mats[s, at, pl.ds(h * 256 + 128, 128)] = jnp.concatenate([low[8:], high[8:]], 0).astype(jnp.bfloat16)
            squares[s] += total

    pending = [(0, h) for h in range(CHUNKS)]
    for k in range(1, hops + 1):
        for h in range(CHUNKS):
            for d in range(2):
                ring_copies[k, d, h].wait_recv()
                if k < hops:
                    send_ring(k + 1, d, h)
            ready = []
            for delta in sorted({k, planes - k}):
                ready.append((delta, h))
            for delta, hh in ready:
                pick(delta, hh)
            while len(pending) > 4:
                place(*pending.pop(0))
            pending += ready
    for copy in factors:
        copy.wait()
    for h in range(CHUNKS):
        for item in [p for p in pending if p[1] == h]:
            place(*item)

        def left_part(s, carry):
            part = jnp.dot(left[s], mats[s, :, pl.ds(h * 256, 256)], preferred_element_type=jnp.float32)
            halves[s, :, pl.ds(h * 256, 256)] = part.astype(jnp.bfloat16)
            return carry

        lax.fori_loop(0, SLOTS, left_part, 0)

    cells = rows * BLK

    def right_part(s, total):
        product = jnp.dot(halves[s], right[s], preferred_element_type=jnp.float32)
        prods[s] = product
        prod_sum = jnp.sum(product * product, keepdims=True)
        grad_sum = jnp.sum(squares[s], keepdims=True)
        scale = jnp.sqrt(grad_sum / cells + EPSILON) / jnp.sqrt(prod_sum / cells + EPSILON)
        scales[s] = jnp.broadcast_to(scale, (8, 128))
        own = tab[BELOW + dp * SLOTS + s]
        found = jnp.full((1, 1), tab[CELL_OF + jnp.minimum(own, nblk - 1)])
        held = found == jnp.full((1, 1), dp * SLOTS + s)
        return total + jnp.where(held, prod_sum * scale * scale, 0.0)

    total = lax.fori_loop(0, SLOTS, right_part, jnp.zeros((1, 1), jnp.float32))
    stages = len(partners)
    sums[0] = jnp.broadcast_to(total, sums.shape[1:])
    sum_copies = []

    def exchange():
        i = len(sum_copies)
        if i:
            sum_copies[i - 1].wait_recv()
            sums[2 * i] = sums[2 * i - 2] + sums[2 * i - 1]
        if i < stages:
            sum_copies.append(
                remote(sums.at[2 * i], sums.at[2 * i + 1], sum_ss.at[i], sum_rs.at[i], partners[i])
            )


    def y_at(delta, h):
        if delta == 0:
            return back_last[h], 2 * capacity[0]
        if delta == hops:
            return back_first[h], 0
        k, d = (delta, 1) if delta < hops else (planes - delta, 0)
        return back[k - 1][d][h], capacity[k]

    def send_y(delta):
        target = plane(delta)
        for s in range(SLOTS):
            scale = scales[s][:, :1]
            for rel in range(NX):
                xx = (x + rel) % NX
                value = prods[s, pl.ds(pl.multiple_of((target * NX + xx) * 8, 8), 8), :] * scale
                for h in range(CHUNKS):
                    part = fold(value[:, h * 256 : (h + 1) * 256])
                    if rel == 0:
                        ref, row = y_at(delta, h)
                        ref[row + x * SLOTS + s] = part
                    else:
                        ys[delta, h, rel - 1, s] = part
        for h in range(CHUNKS):
            ref, row = y_at(delta, h)
            for rel in range(1, NX):
                landing = ref.at[pl.ds(row + x * SLOTS, SLOTS)]
                start(ys.at[delta, h, rel - 1], landing, y_ss.at[0], y_rs.at[delta, h], along[rel])

    waited = set()

    def wait_y(delta, h):
        if (delta, h) not in waited:
            waited.add((delta, h))
            alike = ys.at[delta, h]
            describe(alike, alike, y_ss.at[0], y_rs.at[delta, h], along[1]).wait_recv()

    back_copies = {}

    def send_back(k, d, h):
        if k < hops:
            back_copies[k + 1, d, h].wait_recv()
        delta = planes - k if d == 0 else k
        wait_y(delta, h)
        target_end = tab[ENDS + plane(delta)]
        low = z * CELLS
        width = capacity[k - 1]
        filled = capacity[k] if k < hops else 0

        ref, row = y_at(delta, h)

        def merge(j, keep):
            rank = (target_end - 1 - j if d == 0 else target_end + j) & (nblk - 1)
            local = tab[CELL_OF + rank] - low
            at = row + jnp.clip(local, 0, CELLS - 1)
            if keep:
                at = jnp.where((local >= 0) & (local < CELLS), at, j)
            back_send[k - 1][d][h][j] = ref[at]

        loop(filled, functools.partial(merge, keep=True), 8)
        loop(width - filled, lambda j: merge(filled + j, False), 8)
        if k > 1:
            landing = back[k - 2][d][h].at[pl.ds(0, width)]
        else:
            landing = back_last[h].at[pl.ds(d * width, width)]
        back_copies[k, d, h] = remote(
            back_send[k - 1][d][h], landing,
            back_ss.at[k - 1, d, h], back_rs.at[k - 1, d, h], toward[1 - d],
        )

    points = [(k, h) for k in range(hops - 2, 1, -1) for h in range(CHUNKS)]
    points = (points[:-2] + points[-1:])[:stages]
    sent = set()

    def ensure_y(delta):
        if delta not in sent:
            sent.add(delta)
            send_y(delta)

    for k in range(hops, 0, -1):
        for ahead in range(k, max(k - 3, -1), -1):
            ensure_y((planes - ahead) % planes)
            ensure_y(ahead)
        for h in range(CHUNKS):
            for d in range(2):
                send_back(k, d, h)
            if (k, h) in points:
                exchange()
    ensure_y(0)
    while len(sum_copies) < stages:
        exchange()
    exchange()
    update_rms = jnp.sqrt(sums[2 * stages] / (nblk * cells * tensors) + EPSILON)
    rms_out[0, 0] = update_rms[0, 0]
    inv_rms = (1.0 / update_rms)[:1, :1]

    end = tab[ENDS + z]
    ups = tab[UPS + z]
    for h in range(CHUNKS):
        for d in range(2):
            back_copies[1, d, h].wait_recv()
        wait_y(0, h)

        def finish(b, h=h):
            rank = tab[RANK_OF + b]
            local = tab[CELL_OF + rank] - z * CELLS
            up = (end - 1 - rank) & (nblk - 1)
            down = (rank - end) & (nblk - 1)
            room = capacity[0]
            at = jnp.where(up < ups, jnp.minimum(up, room - 1), room + jnp.minimum(down, room - 1))
            mine = (local >= 0) & (local < CELLS)
            at = jnp.where(mine, 2 * room + jnp.clip(local, 0, CELLS - 1), at)
            value = back_last[h][at].astype(jnp.float32) * inv_rms
            wide = jnp.concatenate([value[:8], value[8:]], axis=1).astype(jnp.bfloat16)
            column = (b % per_row) * BLK + h * 256
            out[b // per_row, :, pl.ds(pl.multiple_of(column, 256), 256)] = wide

        loop(nblk, finish, 8)

    for copy in sends:
        copy.wait_send()
    describe(xs, xs, x_ss.at[0], x_rs.at[0, 0], along[1]).wait_send()
    describe(ys, ys, y_ss.at[0], y_rs.at[0, 0], along[1]).wait_send()


def ring_call(grad, table, left_root, right_root, planes, tensors, capacity):
    row_blocks, piece_rows, width = grad.shape
    nblk = row_blocks * (width // BLK)
    rows = left_root.shape[-1]
    hops = len(capacity)
    tile = (16, 128)
    bf16, f32 = jnp.bfloat16, jnp.float32
    vmem = pltpu.VMEM
    dma = pltpu.SemaphoreType.DMA

    def tiles(*counts):
        return [vmem((count, *tile), bf16) for count in counts for _ in range(CHUNKS)]

    scratch = [
        vmem((SLOTS, rows, rows), bf16),
        vmem((SLOTS, BLK, BLK), bf16),
        vmem((SLOTS, rows, BLK), bf16),
        vmem((SLOTS, rows, BLK), bf16),
        vmem((SLOTS, rows, BLK), f32),
        vmem((SLOTS, 8, 128), f32),
        vmem((SLOTS, *tile), f32),
    ]
    twice = [capacity[k // 2] for k in range(2 * hops)]
    scratch += tiles(nblk)
    scratch += tiles(*twice[:2])
    scratch += tiles(*twice[:-2])
    scratch += tiles(2 * capacity[-1])
    scratch += [vmem((planes, CHUNKS, n, SLOTS, *tile), bf16) for n in (NX - 1, NX, NX - 1)]
    scratch += tiles(*twice)
    scratch += tiles(*[count + CELLS for count in twice[2:]])
    scratch += tiles(CELLS)
    scratch += tiles(2 * capacity[0] + CELLS)
    stages = (planes * NX * tensors).bit_length() - 1
    scratch += [vmem((2 * stages + 1, 8, 128), f32)]
    scratch += [dma((2,))]
    scratch += [dma((hops, 2, CHUNKS))] * 2
    scratch += [dma((1,)), dma((planes, CHUNKS))] * 2
    scratch += [dma((hops, 2, CHUNKS))] * 2
    scratch += [dma((stages,))] * 2
    body = functools.partial(kernel, planes, nblk, capacity)
    in_vmem = pl.BlockSpec(memory_space=pltpu.VMEM)
    return pl.pallas_call(
        body,
        out_shape=(
            jax.ShapeDtypeStruct(grad.shape, bf16),
            jax.ShapeDtypeStruct((1, 1), f32),
        ),
        in_specs=[
            pl.BlockSpec(memory_space=pltpu.SMEM),
            in_vmem,
            pl.BlockSpec(memory_space=pl.ANY),
            pl.BlockSpec(memory_space=pl.ANY),
        ],
        out_specs=(in_vmem, pl.BlockSpec(memory_space=pltpu.SMEM)),
        scratch_shapes=scratch,
        compiler_params=pltpu.CompilerParams(
            collective_id=0, has_side_effects=True, vmem_limit_bytes=50 * 1024 * 1024
        ),
        cost_estimate=pl.CostEstimate(
            flops=4 * SLOTS * rows * rows * BLK, bytes_accessed=4 * 1024 * 1024, transcendentals=0
        ),
        name="sorted_ring",
    )(table, grad, left_root, right_root)


def precondition(block, left_factor, right_factor):
    left_part = jnp.dot(left_factor, block, preferred_element_type=jnp.float32).astype(jnp.bfloat16)
    product = jnp.dot(left_part, right_factor, preferred_element_type=jnp.float32)
    grad_mean = jnp.mean(jnp.square(block.astype(jnp.float32)))
    prod_mean = jnp.mean(jnp.square(product))
    update = product * (jnp.sqrt(grad_mean + EPSILON) / jnp.sqrt(prod_mean + EPSILON))
    return (update, jnp.sum(update * update))


def padded_call(grad, cell, left_root, right_root, dp_size):
    row_blocks, piece_rows, width = grad.shape
    col_blocks = width // BLK
    per_group = row_blocks * col_blocks
    position = (cell % SLOTS) * dp_size + cell // SLOTS
    select = (position[None, :] == jnp.arange(SLOTS * dp_size, dtype=jnp.int32)[:, None]).astype(jnp.bfloat16)
    pieces = (
        grad.reshape(row_blocks, piece_rows, col_blocks, BLK)
        .transpose(0, 2, 1, 3)
        .reshape(per_group, piece_rows * BLK)
    )
    outgoing = jnp.dot(select, pieces, preferred_element_type=jnp.float32).astype(jnp.bfloat16)
    outgoing = outgoing.reshape(SLOTS, dp_size * piece_rows, BLK)
    arrived = lax.all_to_all(outgoing, "dp", split_axis=1, concat_axis=1, tiled=True)
    outcomes = [precondition(arrived[s], left_root[0, s], right_root[0, s]) for s in range(SLOTS)]
    updates = jnp.stack([outcome[0] for outcome in outcomes]).astype(jnp.bfloat16)
    partial_sum = sum([outcome[1] for outcome in outcomes])
    returned = lax.all_to_all(updates, "dp", split_axis=1, concat_axis=1, tiled=True)
    placed = jnp.take(returned.reshape(SLOTS * dp_size, piece_rows * BLK), position, axis=0)
    placed = placed.reshape(row_blocks, col_blocks, piece_rows, BLK).transpose(0, 2, 1, 3)
    cells = per_group * dp_size * piece_rows * BLK * lax.axis_size("tensor")
    update_rms = jnp.sqrt(lax.psum(partial_sum, ("dp", "tensor")) / cells + EPSILON)
    direction = placed.reshape(row_blocks, piece_rows, width).astype(jnp.float32) * (1.0 / update_rms)
    return direction.astype(jnp.bfloat16), update_rms


def per_device(capacity, grad, owner, left_root, right_root):
    row_blocks, piece_rows, width = grad.shape
    dp_size = lax.axis_size("dp")
    tensors = lax.axis_size("tensor")
    planes = dp_size // NX
    col_blocks = width // BLK
    tensor_index = lax.axis_index("tensor")
    here = lax.dynamic_slice_in_dim(owner, tensor_index * col_blocks, col_blocks, 1).reshape(-1)
    ends, ups, fits = plane_split(owner, tensors, planes, capacity)
    cell, rank = block_cells(here)
    ends = lax.dynamic_index_in_dim(ends, tensor_index, 0, keepdims=False)
    ups = lax.dynamic_index_in_dim(ups, tensor_index, 0, keepdims=False)
    table = make_table(cell, rank, ends, ups, dp_size)

    def fast(grad, table, cell, left_root, right_root):
        moved, rms = ring_call(grad, table, left_root, right_root, planes, tensors, capacity)
        return moved, rms.reshape(())

    def padded(grad, table, cell, left_root, right_root):
        return padded_call(grad, cell, left_root, right_root, dp_size)

    return lax.cond(fits, fast, padded, grad, table, cell, left_root, right_root)


def build(mesh, capacity):
    return jax.shard_map(
        functools.partial(per_device, capacity),
        mesh=mesh,
        in_specs=(
            P(None, "dp", "tensor"),
            P(),
            P("tensor", "dp", None, None),
            P("tensor", "dp", None, None),
        ),
        out_specs=(P(None, "dp", "tensor"), P()),
        check_vma=False,
    )


def solution(mesh):
    return build(mesh, CAPACITY)
```

```python
import functools

import jax
import jax.numpy as jnp
from jax import lax
from jax.experimental import pallas as pl
from jax.experimental.pallas import tpu as pltpu
from jax.sharding import PartitionSpec as P

BLK = 512
EPSILON = 1e-06
MESH = pl.DeviceIdType.MESH

NX = 4
SLOTS = 3
CELLS = NX * SLOTS
CHUNKS = 2
BITS = (1, 2, 4, 8, 16, 32)
DISTANCE = ((0, 1, 2, 0, 0, 0), (1, 2, 1, 2, 4, 8))
CAPACITIES = ((38, 34, 30, 25, 20, 15, 10, 5), (42, 37, 34, 28, 24, 19, 12, 7))


def block_cells(owners):
    n = owners.shape[0]
    index = jnp.arange(n, dtype=jnp.int32)
    same = owners[:, None] == owners[None, :]
    slot = jnp.sum((same & (index[None, :] < index[:, None])).astype(jnp.int32), axis=1)
    cell = owners * SLOTS + slot
    rank = jnp.sum((cell[None, :] < cell[:, None]).astype(jnp.int32), axis=1)
    return cell, rank


def plane_split(owner, tensors, planes, capacities):
    z = jnp.arange(planes, dtype=jnp.int32)
    counts = jnp.sum((owner[:, :, None] // NX == z).astype(jnp.float32), axis=0)
    counts = jnp.sum(counts.reshape(tensors, -1, planes), axis=1)
    q = jnp.arange(2 * planes + 1, dtype=jnp.int32)
    turns = (z[:, None] < q[None, :]).astype(jnp.float32) + (z[:, None] + planes < q[None, :]).astype(jnp.float32)
    below = jnp.dot(counts, turns, precision=lax.Precision.HIGHEST).astype(jnp.int32)
    first = below[:, 1 : planes + 1]
    level = jnp.full_like(first, len(capacities))
    ends = first
    for i, capacity in reversed(list(enumerate(capacities))):
        high, low = None, None
        for k, room in enumerate(tuple(capacity) + (0,), 1):
            up = below[:, k : k + planes] + room
            down = below[:, planes + 1 - k : 2 * planes + 1 - k] - room
            high = up if high is None else jnp.minimum(high, up)
            low = down if low is None else jnp.maximum(low, down)
        fits = low <= high
        level = jnp.where(fits, i, level)
        ends = jnp.where(fits, jnp.maximum((high + low) // 2, first), ends)
    return ends, ends - first, jnp.max(level)


def make_table(cell, rank, ends, ups, devices):
    n = cell.shape[0]
    index = jnp.arange(n, dtype=jnp.int32)
    hit = (rank[None, :] == index[:, None]).astype(jnp.int32)
    block_of = jnp.sum(hit * index[None, :], axis=-1)
    cell_of = jnp.sum(hit * cell[None, :], axis=-1)
    cells = jnp.arange(devices * SLOTS, dtype=jnp.int32)
    below = jnp.sum((cell[None, :] < cells[:, None]).astype(jnp.int32), axis=-1)
    return jnp.concatenate([block_of, cell_of, rank, below, ends, ups])


def fold(piece):
    return jnp.concatenate([piece[:, :128], piece[:, 128:]], axis=0).astype(jnp.bfloat16)


def loop(count, body, unroll):
    turns = count // unroll

    def turn(t, carry):
        for u in range(unroll):
            body(t * unroll + u)
        return carry

    if turns:
        lax.fori_loop(0, turns, turn, 0)
    for j in range(turns * unroll, count):
        body(j)


def arrived_slots(capacity):
    return capacity[1:-2] + (capacity[-2] + capacity[-1], 0)


def kernel(planes, nblk, capacity, *refs):
    hops = len(capacity)
    arrivals = arrived_slots(capacity)
    names = iter(refs)

    def take(*shape):
        if not shape:
            return next(names)
        return [take(*shape[1:]) for _ in range(shape[0])]

    tab, grad, left_hbm, right_hbm = take(4)
    out, rms_out = take(2)
    left, right, mats, halves, prods, scales, squares = take(7)
    folded = take(CHUNKS)
    first = take(2, CHUNKS)
    ring = take(hops - 1, 2, CHUNKS)
    ring_last = take(CHUNKS)
    xs, xr, ys = take(3)
    back_send = take()
    back = take(hops - 1, 2, CHUNKS)
    back_first = take(CHUNKS)
    back_last = take(CHUNKS)
    sums = take()
    load_sem, ring_ss, ring_rs, x_ss, x_rs, y_ss, y_rs, back_ss, back_rs, sum_ss, sum_rs = take(11)

    rows = mats.shape[1]
    dp = lax.axis_index("dp")
    tensor = lax.axis_index("tensor")
    tensors = lax.axis_size("tensor")
    z, x = dp // NX, dp % NX
    devices = planes * NX
    per_row = nblk // grad.shape[0]
    CELL_OF, RANK_OF, BELOW = nblk, 2 * nblk, 3 * nblk
    ENDS = BELOW + devices * SLOTS
    UPS = ENDS + planes

    def plane(delta):
        return (z + (delta + planes)) % planes

    def device(zz, xx):
        return (zz * NX + xx, tensor)

    toward = [device(plane(1), x), device(plane(-1), x)]
    toward_two = [device(plane(2), x), device(plane(-2), x)]
    along = [None] + [device(z, (x + rel) % NX) for rel in range(1, NX)]

    factors = [
        pltpu.make_async_copy(left_hbm.at[0], left, load_sem.at[0]),
        pltpu.make_async_copy(right_hbm.at[0], right, load_sem.at[1]),
    ]
    for copy in factors:
        copy.start()

    barrier = pltpu.get_barrier_semaphore()
    partners = []
    bits = [(stride, place) for place, size in ((0, tensors), (1, devices)) for stride in BITS if stride < size]
    for stride, place in sorted(bits, key=lambda bit: (DISTANCE[bit[1]][BITS.index(bit[0])], bit)):
        if place:
            partners.append((dp + stride - 2 * stride * ((dp // stride) % 2), tensor))
        else:
            partners.append((dp, tensor + stride - 2 * stride * ((tensor // stride) % 2)))
    peers = toward + along[1:] + [partner for partner in partners if partner[0] is dp]
    for peer in peers:
        pl.semaphore_signal(barrier, inc=1, device_id=peer, device_id_type=MESH)

    end = tab[ENDS + z]

    def fill_chunk(h):
        def fold_row(r):
            for c in range(per_row):
                piece = grad[r, :, pl.ds(c * BLK + h * 256, 256)].astype(jnp.float32)
                folded[h][r * per_row + c] = fold(piece)

        def fill_first(j):
            first[0][h][j] = folded[h][tab[(end - 1 - j) & (nblk - 1)]]
            first[1][h][j] = folded[h][tab[(end + j) & (nblk - 1)]]

        loop(grad.shape[0], fold_row, 4)
        loop(capacity[0], fill_first, 8)

    fill_chunk(0)
    pl.semaphore_wait(barrier, len(peers))

    sends = []

    def describe(src, dst, ss, rs, target):
        return pltpu.make_async_remote_copy(
            src_ref=src, dst_ref=dst, send_sem=ss, recv_sem=rs, device_id=target, device_id_type=MESH
        )

    def start(*args):
        copy = describe(*args)
        copy.start()
        return copy

    def remote(*args):
        copy = start(*args)
        sends.append(copy)
        return copy

    ring_copies = {}

    def ring_at(k, d, h):
        if k < hops:
            return ring[k - 1][d][h]
        return ring_last[h].at[pl.ds(d * capacity[k - 1], capacity[k - 1])]

    def send_ring(k, d, h):
        last = k == hops
        src = first[d][h] if k == 1 else ring_at(k - 2 if last else k - 1, d, h).at[pl.ds(0, capacity[k - 1])]
        target = toward_two[d] if last else toward[d]
        ring_copies[k, d, h] = start(src, ring_at(k, d, h), ring_ss.at[0], ring_rs.at[k - 1, d, h], target)

    for h in range(CHUNKS):
        if h:
            fill_chunk(h)
        for d in range(2):
            send_ring(1, d, h)

    def send_x(delta, h):
        for rel in range(1, NX):
            start(xs.at[delta, h, rel - 1], xr.at[delta, h, rel], x_ss.at[0], x_rs.at[delta, h], along[rel])

    def put_x(delta, h, rel, s, value):
        if rel == 0:
            xr[delta, h, 0, s] = value
        else:
            xs[delta, h, rel - 1, s] = value

    def cell_index(rel, s):
        return z * CELLS + ((x + rel) % NX) * SLOTS + s

    for rel in range(NX):
        for s in range(SLOTS):
            rank = tab[BELOW + cell_index(rel, s)]
            block = tab[jnp.minimum(rank, nblk - 1)]
            for h in range(CHUNKS):
                put_x(0, h, rel, s, folded[h][block])
    for h in range(CHUNKS):
        send_x(0, h)

    def pick(delta, h):
        source = plane(-delta)
        source_end, source_ups = tab[ENDS + source], tab[UPS + source]
        k = min(delta, planes - delta)
        room = capacity[k - 1]
        for rel in range(NX):
            for s in range(SLOTS):
                rank = tab[BELOW + cell_index(rel, s)]
                up = (source_end - 1 - rank) & (nblk - 1)
                down = (rank - source_end) & (nblk - 1)
                if k == hops:
                    at = jnp.where(up < source_ups, jnp.minimum(up, room - 1), room + jnp.minimum(down, room - 1))
                    value = ring_last[h][at]
                elif delta < hops:
                    value = ring[k - 1][0][h][jnp.minimum(up, room - 1)]
                else:
                    value = ring[k - 1][1][h][jnp.minimum(down, room - 1)]
                put_x(delta, h, rel, s, value)
        send_x(delta, h)

    squares[...] = jnp.zeros_like(squares)

    def place(delta, h):
        arrived = xr.at[delta, h, pl.ds(1, NX - 1)]
        describe(arrived, arrived, x_ss.at[0], x_rs.at[delta, h], along[1]).wait_recv()
        source = plane(-delta)
        for s in range(SLOTS):
            total = None
            for pair in range(NX // 2):
                low, high = (
                    xr[delta, h, (x - (2 * pair + i) + NX) % NX, s].astype(jnp.float32) for i in range(2)
                )
                term = low * low + high * high
                total = term if total is None else total + term
                at = pl.ds(pl.multiple_of(source * (8 * NX) + 16 * pair, 16), 16)
                mats[s, at, pl.ds(h * 256, 128)] = jnp.concatenate([low[:8], high[:8]], 0).astype(jnp.bfloat16)
                mats[s, at, pl.ds(h * 256 + 128, 128)] = jnp.concatenate([low[8:], high[8:]], 0).astype(jnp.bfloat16)
            squares[s] += total

    pending = [(0, h) for h in range(CHUNKS)]
    for k in range(1, hops + 1):
        for h in range(CHUNKS):
            for d in range(2):
                ring_copies[k, d, h].wait_recv()
                if k < hops - 1:
                    send_ring(k + 1, d, h)
                if k == hops - 2:
                    send_ring(hops, d, h)
            ready = []
            for delta in sorted({k, planes - k}):
                ready.append((delta, h))
            for delta, hh in ready:
                pick(delta, hh)
            while len(pending) > 4:
                place(*pending.pop(0))
            pending += ready
    for copy in factors:
        copy.wait()
    for h in range(CHUNKS):
        for item in [p for p in pending if p[1] == h]:
            place(*item)

        def left_part(s, carry):
            part = jnp.dot(left[s], mats[s, :, pl.ds(h * 256, 256)], preferred_element_type=jnp.float32)
            halves[s, :, pl.ds(h * 256, 256)] = part.astype(jnp.bfloat16)
            return carry

        lax.fori_loop(0, SLOTS, left_part, 0)

    cells = rows * BLK

    def right_part(s, total):
        product = jnp.dot(halves[s], right[s], preferred_element_type=jnp.float32)
        prods[s] = product
        prod_sum = jnp.sum(product * product, keepdims=True)
        grad_sum = jnp.sum(squares[s], keepdims=True)
        scale = jnp.sqrt(grad_sum / cells + EPSILON) / jnp.sqrt(prod_sum / cells + EPSILON)
        scales[s] = jnp.broadcast_to(scale, (8, 128))
        own = tab[BELOW + dp * SLOTS + s]
        found = jnp.full((1, 1), tab[CELL_OF + jnp.minimum(own, nblk - 1)])
        held = found == jnp.full((1, 1), dp * SLOTS + s)
        return total + jnp.where(held, prod_sum * scale * scale, 0.0)

    total = lax.fori_loop(0, SLOTS, right_part, jnp.zeros((1, 1), jnp.float32))
    stages = len(partners)
    sums[0] = jnp.broadcast_to(total, sums.shape[1:])
    sum_copies = []

    def exchange():
        i = len(sum_copies)
        if i:
            sum_copies[i - 1].wait_recv()
            sums[2 * i] = sums[2 * i - 2] + sums[2 * i - 1]
        if i < stages:
            sum_copies.append(
                remote(sums.at[2 * i], sums.at[2 * i + 1], sum_ss.at[i], sum_rs.at[i], partners[i])
            )


    def y_at(delta, h):
        if delta == 0:
            return back_last[h], 2 * capacity[0]
        if delta == hops:
            return back_first[h], 0
        k, d = (delta, 1) if delta < hops else (planes - delta, 0)
        return back[k - 1][d][h], arrivals[k - 1]

    def send_y(delta):
        target = plane(delta)
        for s in range(SLOTS):
            scale = scales[s][:, :1]
            for rel in range(NX):
                xx = (x + rel) % NX
                value = prods[s, pl.ds(pl.multiple_of((target * NX + xx) * 8, 8), 8), :] * scale
                for h in range(CHUNKS):
                    part = fold(value[:, h * 256 : (h + 1) * 256])
                    if rel == 0:
                        ref, row = y_at(delta, h)
                        ref[row + x * SLOTS + s] = part
                    else:
                        ys[delta, h, rel - 1, s] = part
        for h in range(CHUNKS):
            ref, row = y_at(delta, h)
            for rel in range(1, NX):
                landing = ref.at[pl.ds(row + x * SLOTS, SLOTS)]
                start(ys.at[delta, h, rel - 1], landing, y_ss.at[0], y_rs.at[delta, h], along[rel])

    waited = set()

    def wait_y(delta, h):
        if (delta, h) not in waited:
            waited.add((delta, h))
            alike = ys.at[delta, h]
            describe(alike, alike, y_ss.at[0], y_rs.at[delta, h], along[1]).wait_recv()

    back_copies = {}
    cells_all = planes * CELLS

    def send_back(k, d, h):
        for farther in [k + 1] * (k < hops - 1) + [hops] * (k == hops - 2):
            back_copies[farther, d, h].wait_recv()
        delta = planes - k if d == 0 else k
        wait_y(delta, h)
        target_end = tab[ENDS + plane(delta)]
        low = z * CELLS
        width = capacity[k - 1]
        filled = capacity[k] if k < hops - 1 else 0
        ref, row = y_at(delta, h)
        offset = sum(capacity[: k - 1]) * 2 * CHUNKS + (d * CHUNKS + h) * width

        def merge(j, keep):
            rank = (target_end - 1 - j if d == 0 else target_end + j) & (nblk - 1)
            local = tab[CELL_OF + rank] - low
            at = row + jnp.clip(local, 0, CELLS - 1)
            if keep:
                other = j
                if k == hops - 2:
                    away = lax.rem(local + cells_all, cells_all)
                    away = away - 2 * CELLS if d == 0 else cells_all - 1 - away - CELLS
                    two = (away >= 0) & (away < CELLS)
                    other = jnp.where(two, filled + jnp.minimum(j, capacity[k + 1] - 1), j)
                at = jnp.where((local >= 0) & (local < CELLS), at, other)
            back_send[offset + j] = ref[at]

        loop(filled, functools.partial(merge, keep=True), 8)
        loop(width - filled, lambda j: merge(filled + j, False), 8)
        if k == hops:
            landing = back[k - 3][d][h].at[pl.ds(capacity[k - 2], width)]
        elif k > 1:
            landing = back[k - 2][d][h].at[pl.ds(0, width)]
        else:
            landing = back_last[h].at[pl.ds(d * width, width)]
        target = toward_two[1 - d] if k == hops else toward[1 - d]
        source = back_send.at[pl.ds(offset, width)]
        back_copies[k, d, h] = start(source, landing, back_ss.at[0], back_rs.at[k - 1, d, h], target)

    points = [(k, h) for k in range(hops - 2, 1, -1) for h in range(CHUNKS)]
    points = (points[:-2] + points[-1:])[:stages]
    sent = set()

    def ensure_y(delta):
        if delta not in sent:
            sent.add(delta)
            send_y(delta)

    for k in range(hops, 0, -1):
        for ahead in range(k, max(k - 3, -1), -1):
            ensure_y((planes - ahead) % planes)
            ensure_y(ahead)
        for h in range(CHUNKS):
            for d in range(2):
                send_back(k, d, h)
            if (k, h) in points:
                exchange()
    ensure_y(0)
    while len(sum_copies) < stages:
        exchange()
    exchange()
    update_rms = jnp.sqrt(sums[2 * stages] / (nblk * cells * tensors) + EPSILON)
    rms_out[0, 0] = update_rms[0, 0]
    inv_rms = (1.0 / update_rms)[:1, :1]

    end = tab[ENDS + z]
    ups = tab[UPS + z]
    for h in range(CHUNKS):
        for d in range(2):
            back_copies[1, d, h].wait_recv()
        wait_y(0, h)

        def finish(b, h=h):
            rank = tab[RANK_OF + b]
            local = tab[CELL_OF + rank] - z * CELLS
            up = (end - 1 - rank) & (nblk - 1)
            down = (rank - end) & (nblk - 1)
            room = capacity[0]
            at = jnp.where(up < ups, jnp.minimum(up, room - 1), room + jnp.minimum(down, room - 1))
            mine = (local >= 0) & (local < CELLS)
            at = jnp.where(mine, 2 * room + jnp.clip(local, 0, CELLS - 1), at)
            value = back_last[h][at].astype(jnp.float32) * inv_rms
            wide = jnp.concatenate([value[:8], value[8:]], axis=1).astype(jnp.bfloat16)
            column = (b % per_row) * BLK + h * 256
            out[b // per_row, :, pl.ds(pl.multiple_of(column, 256), 256)] = wide

        loop(nblk, finish, 8)

    for copy in sends:
        copy.wait_send()
    describe(xs, xs, x_ss.at[0], x_rs.at[0, 0], along[1]).wait_send()
    describe(ys, ys, y_ss.at[0], y_rs.at[0, 0], along[1]).wait_send()
    describe(back_send, back_send, ring_ss.at[0], ring_rs.at[0, 0, 0], toward[0]).wait_send()
    describe(back_send, back_send, back_ss.at[0], back_rs.at[0, 0, 0], toward[0]).wait_send()


def ring_call(grad, table, left_root, right_root, planes, tensors, capacity, number):
    row_blocks, piece_rows, width = grad.shape
    nblk = row_blocks * (width // BLK)
    rows = left_root.shape[-1]
    hops = len(capacity)
    tile = (16, 128)
    bf16, f32 = jnp.bfloat16, jnp.float32
    vmem = pltpu.VMEM
    dma = pltpu.SemaphoreType.DMA

    def tiles(*counts):
        return [vmem((count, *tile), bf16) for count in counts for _ in range(CHUNKS)]

    scratch = [
        vmem((SLOTS, rows, rows), bf16),
        vmem((SLOTS, BLK, BLK), bf16),
        vmem((SLOTS, rows, BLK), bf16),
        vmem((SLOTS, rows, BLK), bf16),
        vmem((SLOTS, rows, BLK), f32),
        vmem((SLOTS, 8, 128), f32),
        vmem((SLOTS, *tile), f32),
    ]
    twice = [capacity[k // 2] for k in range(2 * hops)]
    scratch += tiles(nblk)
    scratch += tiles(*twice[:2])
    scratch += tiles(*twice[:-2])
    scratch += tiles(2 * capacity[-1])
    scratch += [vmem((planes, CHUNKS, n, SLOTS, *tile), bf16) for n in (NX - 1, NX, NX - 1)]
    scratch += [vmem((2 * CHUNKS * sum(capacity), *tile), bf16)]
    scratch += tiles(*[count + CELLS for count in arrived_slots(capacity) for _ in range(2)])
    scratch += tiles(CELLS)
    scratch += tiles(2 * capacity[0] + CELLS)
    stages = (planes * NX * tensors).bit_length() - 1
    scratch += [vmem((2 * stages + 1, 8, 128), f32)]
    scratch += [dma((2,))]
    scratch += [dma((1,)), dma((hops, 2, CHUNKS))]
    scratch += [dma((1,)), dma((planes, CHUNKS))] * 2
    scratch += [dma((1,)), dma((hops, 2, CHUNKS))]
    scratch += [dma((stages,))] * 2
    body = functools.partial(kernel, planes, nblk, capacity)
    in_vmem = pl.BlockSpec(memory_space=pltpu.VMEM)
    return pl.pallas_call(
        body,
        out_shape=(
            jax.ShapeDtypeStruct(grad.shape, bf16),
            jax.ShapeDtypeStruct((1, 1), f32),
        ),
        in_specs=[
            pl.BlockSpec(memory_space=pltpu.SMEM),
            in_vmem,
            pl.BlockSpec(memory_space=pl.ANY),
            pl.BlockSpec(memory_space=pl.ANY),
        ],
        out_specs=(in_vmem, pl.BlockSpec(memory_space=pltpu.SMEM)),
        scratch_shapes=scratch,
        compiler_params=pltpu.CompilerParams(
            collective_id=number, has_side_effects=True, vmem_limit_bytes=50 * 1024 * 1024
        ),
        cost_estimate=pl.CostEstimate(
            flops=4 * SLOTS * rows * rows * BLK, bytes_accessed=4 * 1024 * 1024, transcendentals=0
        ),
        name=f"sorted_ring_{number}",
    )(table, grad, left_root, right_root)


def precondition(block, left_factor, right_factor):
    left_part = jnp.dot(left_factor, block, preferred_element_type=jnp.float32).astype(jnp.bfloat16)
    product = jnp.dot(left_part, right_factor, preferred_element_type=jnp.float32)
    grad_mean = jnp.mean(jnp.square(block.astype(jnp.float32)))
    prod_mean = jnp.mean(jnp.square(product))
    update = product * (jnp.sqrt(grad_mean + EPSILON) / jnp.sqrt(prod_mean + EPSILON))
    return (update, jnp.sum(update * update))


def padded_call(grad, cell, left_root, right_root, dp_size):
    row_blocks, piece_rows, width = grad.shape
    col_blocks = width // BLK
    per_group = row_blocks * col_blocks
    position = (cell % SLOTS) * dp_size + cell // SLOTS
    select = (position[None, :] == jnp.arange(SLOTS * dp_size, dtype=jnp.int32)[:, None]).astype(jnp.bfloat16)
    pieces = (
        grad.reshape(row_blocks, piece_rows, col_blocks, BLK)
        .transpose(0, 2, 1, 3)
        .reshape(per_group, piece_rows * BLK)
    )
    outgoing = jnp.dot(select, pieces, preferred_element_type=jnp.float32).astype(jnp.bfloat16)
    outgoing = outgoing.reshape(SLOTS, dp_size * piece_rows, BLK)
    arrived = lax.all_to_all(outgoing, "dp", split_axis=1, concat_axis=1, tiled=True)
    outcomes = [precondition(arrived[s], left_root[0, s], right_root[0, s]) for s in range(SLOTS)]
    updates = jnp.stack([outcome[0] for outcome in outcomes]).astype(jnp.bfloat16)
    partial_sum = sum([outcome[1] for outcome in outcomes])
    returned = lax.all_to_all(updates, "dp", split_axis=1, concat_axis=1, tiled=True)
    placed = jnp.take(returned.reshape(SLOTS * dp_size, piece_rows * BLK), position, axis=0)
    placed = placed.reshape(row_blocks, col_blocks, piece_rows, BLK).transpose(0, 2, 1, 3)
    cells = per_group * dp_size * piece_rows * BLK * lax.axis_size("tensor")
    update_rms = jnp.sqrt(lax.psum(partial_sum, ("dp", "tensor")) / cells + EPSILON)
    direction = placed.reshape(row_blocks, piece_rows, width).astype(jnp.float32) * (1.0 / update_rms)
    return direction.astype(jnp.bfloat16), update_rms


def per_device(capacities, grad, owner, left_root, right_root):
    row_blocks, piece_rows, width = grad.shape
    dp_size = lax.axis_size("dp")
    tensors = lax.axis_size("tensor")
    planes = dp_size // NX
    col_blocks = width // BLK
    tensor_index = lax.axis_index("tensor")
    here = lax.dynamic_slice_in_dim(owner, tensor_index * col_blocks, col_blocks, 1).reshape(-1)
    ends, ups, level = plane_split(owner, tensors, planes, capacities)
    cell, rank = block_cells(here)
    ends = lax.dynamic_index_in_dim(ends, tensor_index, 0, keepdims=False)
    ups = lax.dynamic_index_in_dim(ups, tensor_index, 0, keepdims=False)
    table = make_table(cell, rank, ends, ups, dp_size)

    def sorted_lists(number, grad, table, cell, left_root, right_root):
        moved, rms = ring_call(grad, table, left_root, right_root, planes, tensors, capacities[number], number)
        return moved, rms.reshape(())

    def padded(grad, table, cell, left_root, right_root):
        return padded_call(grad, cell, left_root, right_root, dp_size)

    branches = [functools.partial(sorted_lists, number) for number in range(len(capacities))] + [padded]
    return lax.switch(level, branches, grad, table, cell, left_root, right_root)


def build(mesh, capacities):
    return jax.shard_map(
        functools.partial(per_device, capacities),
        mesh=mesh,
        in_specs=(
            P(None, "dp", "tensor"),
            P(),
            P("tensor", "dp", None, None),
            P("tensor", "dp", None, None),
        ),
        out_specs=(P(None, "dp", "tensor"), P()),
        check_vma=False,
    )


def solution(mesh):
    return build(mesh, CAPACITIES)
```

```python
import functools

import jax
import jax.numpy as jnp
from jax import lax
from jax.experimental import pallas as pl
from jax.experimental.pallas import tpu as pltpu
from jax.sharding import PartitionSpec as P

BLK = 512
EPSILON = 1e-06
MESH = pl.DeviceIdType.MESH

NX = 4
SLOTS = 3
CELLS = NX * SLOTS
CHUNKS = 2
BITS = (1, 2, 4, 8, 16, 32)
CAPACITIES = ((38, 34, 30, 25, 20, 15, 10, 5), (42, 37, 34, 28, 24, 19, 12, 7))


def block_cells(owners):
    n = owners.shape[0]
    index = jnp.arange(n, dtype=jnp.int32)
    same = owners[:, None] == owners[None, :]
    slot = jnp.sum((same & (index[None, :] < index[:, None])).astype(jnp.int32), axis=1)
    cell = owners * SLOTS + slot
    rank = jnp.sum((cell[None, :] < cell[:, None]).astype(jnp.int32), axis=1)
    return cell, rank


def plane_split(owner, tensors, planes, capacities):
    z = jnp.arange(planes, dtype=jnp.int32)
    counts = jnp.sum((owner[:, :, None] // NX == z).astype(jnp.float32), axis=0)
    counts = jnp.sum(counts.reshape(tensors, -1, planes), axis=1)
    q = jnp.arange(2 * planes + 1, dtype=jnp.int32)
    turns = (z[:, None] < q[None, :]).astype(jnp.float32) + (z[:, None] + planes < q[None, :]).astype(jnp.float32)
    below = jnp.dot(counts, turns, precision=lax.Precision.HIGHEST).astype(jnp.int32)
    first = below[:, 1 : planes + 1]
    level = jnp.full_like(first, len(capacities))
    ends = first
    for i, capacity in reversed(list(enumerate(capacities))):
        high, low = None, None
        for k, room in enumerate(tuple(capacity) + (0,), 1):
            up = below[:, k : k + planes] + room
            down = below[:, planes + 1 - k : 2 * planes + 1 - k] - room
            high = up if high is None else jnp.minimum(high, up)
            low = down if low is None else jnp.maximum(low, down)
        fits = low <= high
        level = jnp.where(fits, i, level)
        ends = jnp.where(fits, jnp.maximum((high + low) // 2, first), ends)
    return ends, ends - first, jnp.max(level)


def make_table(cell, rank, ends, ups, devices):
    n = cell.shape[0]
    index = jnp.arange(n, dtype=jnp.int32)
    hit = (rank[None, :] == index[:, None]).astype(jnp.int32)
    block_of = jnp.sum(hit * index[None, :], axis=-1)
    cell_of = jnp.sum(hit * cell[None, :], axis=-1)
    cells = jnp.arange(devices * SLOTS, dtype=jnp.int32)
    below = jnp.sum((cell[None, :] < cells[:, None]).astype(jnp.int32), axis=-1)
    return jnp.concatenate([block_of, cell_of, rank, below, ends, ups])


def fold(piece):
    return jnp.concatenate([piece[:, :128], piece[:, 128:]], axis=0).astype(jnp.bfloat16)


def loop(count, body, unroll):
    turns = count // unroll

    def turn(t, carry):
        for u in range(unroll):
            body(t * unroll + u)
        return carry

    if turns:
        lax.fori_loop(0, turns, turn, 0)
    for j in range(turns * unroll, count):
        body(j)


def arrived_slots(capacity):
    return capacity[1:-2] + (capacity[-2] + capacity[-1], 0)


def kernel(planes, nblk, capacity, *refs):
    hops = len(capacity)
    arrivals = arrived_slots(capacity)
    names = iter(refs)

    def take(*shape):
        if not shape:
            return next(names)
        return [take(*shape[1:]) for _ in range(shape[0])]

    tab_hbm, grad_hbm, left_hbm, right_hbm = take(4)
    out, rms_out = take(2)
    tab, grad, left, right, mats, halves, prods, scales, squares = take(9)
    folded = take(CHUNKS)
    first = take(2, CHUNKS)
    ring = take(hops - 1, 2, CHUNKS)
    ring_last = take(CHUNKS)
    xs, xr, ys = take(3)
    back_send = take()
    back = take(hops - 1, 2, CHUNKS)
    back_first = take(CHUNKS)
    back_last = take(CHUNKS)
    sums = take()
    load_sem, ring_ss, ring_rs, x_ss, x_rs, y_ss, y_rs, back_ss, back_rs, sum_ss, sum_rs = take(11)

    rows = mats.shape[1]
    dp = lax.axis_index("dp")
    tensor = lax.axis_index("tensor")
    tensors = lax.axis_size("tensor")
    z, x = dp // NX, dp % NX
    devices = planes * NX
    per_row = nblk // grad.shape[0]
    CELL_OF, RANK_OF, BELOW = nblk, 2 * nblk, 3 * nblk
    ENDS = BELOW + devices * SLOTS
    UPS = ENDS + planes

    def plane(delta):
        return (z + (delta + planes)) % planes

    def device(zz, xx):
        return (zz * NX + xx, tensor)

    toward = [device(plane(1), x), device(plane(-1), x)]
    toward_two = [device(plane(2), x), device(plane(-2), x)]
    along = [None] + [device(z, (x + rel) % NX) for rel in range(1, NX)]

    factors = [
        pltpu.make_async_copy(left_hbm.at[0], left, load_sem.at[0]),
        pltpu.make_async_copy(right_hbm.at[0], right, load_sem.at[1]),
    ]
    inputs = [
        pltpu.make_async_copy(tab_hbm, tab, load_sem.at[2]),
        pltpu.make_async_copy(grad_hbm, grad, load_sem.at[3]),
    ]
    for copy in inputs + factors:
        copy.start()

    barrier = pltpu.get_barrier_semaphore()
    partners = []
    bits = [(place, stride) for place, size in ((0, tensors), (1, devices)) for stride in BITS if stride < size]
    for place, stride in reversed(bits):
        if place:
            partners.append((dp + stride - 2 * stride * ((dp // stride) % 2), tensor))
        else:
            partners.append((dp, tensor + stride - 2 * stride * ((tensor // stride) % 2)))
    peers = toward + along[1:] + [partner for partner in partners if partner[0] is dp]
    for peer in peers:
        pl.semaphore_signal(barrier, inc=1, device_id=peer, device_id_type=MESH)

    for copy in inputs:
        copy.wait()
    end = tab[ENDS + z]

    def fill_chunk(h):
        def fold_row(r):
            for c in range(per_row):
                piece = grad[r, :, pl.ds(c * BLK + h * 256, 256)].astype(jnp.float32)
                folded[h][r * per_row + c] = fold(piece)

        def fill_first(j):
            first[0][h][j] = folded[h][tab[(end - 1 - j) & (nblk - 1)]]
            first[1][h][j] = folded[h][tab[(end + j) & (nblk - 1)]]

        loop(grad.shape[0], fold_row, 4)
        loop(capacity[0], fill_first, 8)

    fill_chunk(0)
    pl.semaphore_wait(barrier, len(peers))

    sends = []

    def describe(src, dst, ss, rs, target):
        return pltpu.make_async_remote_copy(
            src_ref=src, dst_ref=dst, send_sem=ss, recv_sem=rs, device_id=target, device_id_type=MESH
        )

    def start(*args):
        copy = describe(*args)
        copy.start()
        return copy

    def remote(*args):
        copy = start(*args)
        sends.append(copy)
        return copy

    ring_copies = {}

    def ring_at(k, d, h):
        if k < hops:
            return ring[k - 1][d][h]
        return ring_last[h].at[pl.ds(d * capacity[k - 1], capacity[k - 1])]

    def send_ring(k, d, h):
        last = k == hops
        src = first[d][h] if k == 1 else ring_at(k - 2 if last else k - 1, d, h).at[pl.ds(0, capacity[k - 1])]
        target = toward_two[d] if last else toward[d]
        ring_copies[k, d, h] = start(src, ring_at(k, d, h), ring_ss.at[0], ring_rs.at[k - 1, d, h], target)

    for h in range(CHUNKS):
        if h:
            fill_chunk(h)
        for d in range(2):
            send_ring(1, d, h)

    def send_x(delta, h):
        for rel in range(1, NX):
            start(xs.at[delta, h, rel - 1], xr.at[delta, h, rel], x_ss.at[0], x_rs.at[delta, h], along[rel])

    def put_x(delta, h, rel, s, value):
        if rel == 0:
            xr[delta, h, 0, s] = value
        else:
            xs[delta, h, rel - 1, s] = value

    def cell_index(rel, s):
        return z * CELLS + ((x + rel) % NX) * SLOTS + s

    for rel in range(NX):
        for s in range(SLOTS):
            rank = tab[BELOW + cell_index(rel, s)]
            block = tab[jnp.minimum(rank, nblk - 1)]
            for h in range(CHUNKS):
                put_x(0, h, rel, s, folded[h][block])
    for h in range(CHUNKS):
        send_x(0, h)

    def pick(delta, h):
        source = plane(-delta)
        source_end, source_ups = tab[ENDS + source], tab[UPS + source]
        k = min(delta, planes - delta)
        room = capacity[k - 1]
        for rel in range(NX):
            for s in range(SLOTS):
                rank = tab[BELOW + cell_index(rel, s)]
                up = (source_end - 1 - rank) & (nblk - 1)
                down = (rank - source_end) & (nblk - 1)
                if k == hops:
                    at = jnp.where(up < source_ups, jnp.minimum(up, room - 1), room + jnp.minimum(down, room - 1))
                    value = ring_last[h][at]
                elif delta < hops:
                    value = ring[k - 1][0][h][jnp.minimum(up, room - 1)]
                else:
                    value = ring[k - 1][1][h][jnp.minimum(down, room - 1)]
                put_x(delta, h, rel, s, value)
        send_x(delta, h)

    squares[...] = jnp.zeros_like(squares)

    def place(delta, h):
        arrived = xr.at[delta, h, pl.ds(1, NX - 1)]
        describe(arrived, arrived, x_ss.at[0], x_rs.at[delta, h], along[1]).wait_recv()
        source = plane(-delta)
        for s in range(SLOTS):
            total = None
            for pair in range(NX // 2):
                low, high = (
                    xr[delta, h, (x - (2 * pair + i) + NX) % NX, s].astype(jnp.float32) for i in range(2)
                )
                term = low * low + high * high
                total = term if total is None else total + term
                at = pl.ds(pl.multiple_of(source * (8 * NX) + 16 * pair, 16), 16)
                mats[s, at, pl.ds(h * 256, 128)] = jnp.concatenate([low[:8], high[:8]], 0).astype(jnp.bfloat16)
                mats[s, at, pl.ds(h * 256 + 128, 128)] = jnp.concatenate([low[8:], high[8:]], 0).astype(jnp.bfloat16)
            squares[s] += total

    pending = [(0, h) for h in range(CHUNKS)]
    for k in range(1, hops + 1):
        for h in range(CHUNKS):
            for d in range(2):
                ring_copies[k, d, h].wait_recv()
                if k < hops - 1:
                    send_ring(k + 1, d, h)
                if k == hops - 2:
                    send_ring(hops, d, h)
            ready = []
            for delta in sorted({k, planes - k}):
                ready.append((delta, h))
            for delta, hh in ready:
                pick(delta, hh)
            while len(pending) > 4:
                place(*pending.pop(0))
            pending += ready
    for copy in factors:
        copy.wait()
    for h in range(CHUNKS):
        for item in [p for p in pending if p[1] == h]:
            place(*item)

        def left_part(s, carry):
            part = jnp.dot(left[s], mats[s, :, pl.ds(h * 256, 256)], preferred_element_type=jnp.float32)
            halves[s, :, pl.ds(h * 256, 256)] = part.astype(jnp.bfloat16)
            return carry

        for s in range(SLOTS):
            left_part(s, 0)

    cells = rows * BLK

    def right_part(s, total):
        product = jnp.dot(halves[s], right[s], preferred_element_type=jnp.float32)
        prods[s] = product
        prod_sum = jnp.sum(product * product, keepdims=True)
        grad_sum = jnp.sum(squares[s], keepdims=True)
        scale = jnp.sqrt(grad_sum / cells + EPSILON) / jnp.sqrt(prod_sum / cells + EPSILON)
        scales[s] = jnp.broadcast_to(scale, (8, 128))
        own = tab[BELOW + dp * SLOTS + s]
        found = jnp.full((1, 1), tab[CELL_OF + jnp.minimum(own, nblk - 1)])
        held = found == jnp.full((1, 1), dp * SLOTS + s)
        return total + jnp.where(held, prod_sum * scale * scale, 0.0)

    total = jnp.zeros((1, 1), jnp.float32)
    for s in range(SLOTS):
        total = right_part(s, total)
    stages = len(partners)
    sums[0] = jnp.broadcast_to(total, sums.shape[1:])
    sum_copies = []

    def exchange():
        i = len(sum_copies)
        if i:
            sum_copies[i - 1].wait_recv()
            sums[2 * i] = sums[2 * i - 2] + sums[2 * i - 1]
        if i < stages:
            sum_copies.append(
                remote(sums.at[2 * i], sums.at[2 * i + 1], sum_ss.at[i], sum_rs.at[i], partners[i])
            )


    def y_at(delta, h):
        if delta == 0:
            return back_last[h], 2 * capacity[0]
        if delta == hops:
            return back_first[h], 0
        k, d = (delta, 1) if delta < hops else (planes - delta, 0)
        return back[k - 1][d][h], arrivals[k - 1]

    def send_y(delta):
        target = plane(delta)
        for s in range(SLOTS):
            scale = scales[s][:, :1]
            for rel in range(NX):
                xx = (x + rel) % NX
                value = prods[s, pl.ds(pl.multiple_of((target * NX + xx) * 8, 8), 8), :] * scale
                for h in range(CHUNKS):
                    part = fold(value[:, h * 256 : (h + 1) * 256])
                    if rel == 0:
                        ref, row = y_at(delta, h)
                        ref[row + x * SLOTS + s] = part
                    else:
                        ys[delta, h, rel - 1, s] = part
        for h in range(CHUNKS):
            ref, row = y_at(delta, h)
            for rel in range(1, NX):
                landing = ref.at[pl.ds(row + x * SLOTS, SLOTS)]
                start(ys.at[delta, h, rel - 1], landing, y_ss.at[0], y_rs.at[delta, h], along[rel])

    waited = set()

    def wait_y(delta, h):
        if (delta, h) not in waited:
            waited.add((delta, h))
            alike = ys.at[delta, h]
            describe(alike, alike, y_ss.at[0], y_rs.at[delta, h], along[1]).wait_recv()

    back_copies = {}
    cells_all = planes * CELLS

    def send_back(k, d, h):
        for farther in [k + 1] * (k < hops - 1) + [hops] * (k == hops - 2):
            back_copies[farther, d, h].wait_recv()
        delta = planes - k if d == 0 else k
        wait_y(delta, h)
        target_end = tab[ENDS + plane(delta)]
        low = z * CELLS
        width = capacity[k - 1]
        filled = capacity[k] if k < hops - 1 else 0
        ref, row = y_at(delta, h)
        offset = sum(capacity[: k - 1]) * 2 * CHUNKS + (d * CHUNKS + h) * width

        def merge(j, keep):
            rank = (target_end - 1 - j if d == 0 else target_end + j) & (nblk - 1)
            local = tab[CELL_OF + rank] - low
            at = row + jnp.clip(local, 0, CELLS - 1)
            if keep:
                other = j
                if k == hops - 2:
                    away = lax.rem(local + cells_all, cells_all)
                    away = away - 2 * CELLS if d == 0 else cells_all - 1 - away - CELLS
                    two = (away >= 0) & (away < CELLS)
                    other = jnp.where(two, filled + jnp.minimum(j, capacity[k + 1] - 1), j)
                at = jnp.where((local >= 0) & (local < CELLS), at, other)
            back_send[offset + j] = ref[at]

        loop(filled, functools.partial(merge, keep=True), 8)
        loop(width - filled, lambda j: merge(filled + j, False), 8)
        if k == hops:
            landing = back[k - 3][d][h].at[pl.ds(capacity[k - 2], width)]
        elif k > 1:
            landing = back[k - 2][d][h].at[pl.ds(0, width)]
        else:
            landing = back_last[h].at[pl.ds(d * width, width)]
        target = toward_two[1 - d] if k == hops else toward[1 - d]
        source = back_send.at[pl.ds(offset, width)]
        back_copies[k, d, h] = start(source, landing, back_ss.at[0], back_rs.at[k - 1, d, h], target)

    points = [(hops, 0)] + [(k, 1) for k in range(hops - 2, max(hops - 5, 0), -1)]
    points += [(k, h) for k in range(hops - 5, 0, -1) for h in range(CHUNKS)]
    points = points[:stages]
    sent = set()

    def ensure_y(delta):
        if delta not in sent:
            sent.add(delta)
            send_y(delta)

    for k in range(hops, 0, -1):
        for ahead in range(k, max(k - 3, -1), -1):
            ensure_y((planes - ahead) % planes)
            ensure_y(ahead)
        for h in range(CHUNKS):
            for d in range(2):
                send_back(k, d, h)
            if (k, h) in points:
                exchange()
    ensure_y(0)
    while len(sum_copies) < stages:
        exchange()
    exchange()
    update_rms = jnp.sqrt(sums[2 * stages] / (nblk * cells * tensors) + EPSILON)
    rms_out[0, 0] = update_rms[0, 0]
    inv_rms = (1.0 / update_rms)[:1, :1]

    end = tab[ENDS + z]
    ups = tab[UPS + z]
    for h in range(CHUNKS):
        for d in range(2):
            back_copies[1, d, h].wait_recv()
        wait_y(0, h)

        def finish(b, h=h):
            rank = tab[RANK_OF + b]
            local = tab[CELL_OF + rank] - z * CELLS
            up = (end - 1 - rank) & (nblk - 1)
            down = (rank - end) & (nblk - 1)
            room = capacity[0]
            at = jnp.where(up < ups, jnp.minimum(up, room - 1), room + jnp.minimum(down, room - 1))
            mine = (local >= 0) & (local < CELLS)
            at = jnp.where(mine, 2 * room + jnp.clip(local, 0, CELLS - 1), at)
            value = back_last[h][at].astype(jnp.float32) * inv_rms
            wide = jnp.concatenate([value[:8], value[8:]], axis=1).astype(jnp.bfloat16)
            column = (b % per_row) * BLK + h * 256
            out[b // per_row, :, pl.ds(pl.multiple_of(column, 256), 256)] = wide

        loop(nblk, finish, 8)

    for copy in sends:
        copy.wait_send()
    describe(xs, xs, x_ss.at[0], x_rs.at[0, 0], along[1]).wait_send()
    describe(ys, ys, y_ss.at[0], y_rs.at[0, 0], along[1]).wait_send()
    describe(back_send, back_send, ring_ss.at[0], ring_rs.at[0, 0, 0], toward[0]).wait_send()
    describe(back_send, back_send, back_ss.at[0], back_rs.at[0, 0, 0], toward[0]).wait_send()


def ring_call(grad, table, left_root, right_root, planes, tensors, capacity, number):
    row_blocks, piece_rows, width = grad.shape
    nblk = row_blocks * (width // BLK)
    rows = left_root.shape[-1]
    hops = len(capacity)
    tile = (16, 128)
    bf16, f32 = jnp.bfloat16, jnp.float32
    vmem = pltpu.VMEM
    dma = pltpu.SemaphoreType.DMA

    def tiles(*counts):
        return [vmem((count, *tile), bf16) for count in counts for _ in range(CHUNKS)]

    scratch = [
        pltpu.SMEM(table.shape, jnp.int32),
        vmem(grad.shape, bf16),
        vmem((SLOTS, rows, rows), bf16),
        vmem((SLOTS, BLK, BLK), bf16),
        vmem((SLOTS, rows, BLK), bf16),
        vmem((SLOTS, rows, BLK), bf16),
        vmem((SLOTS, rows, BLK), f32),
        vmem((SLOTS, 8, 128), f32),
        vmem((SLOTS, *tile), f32),
    ]
    twice = [capacity[k // 2] for k in range(2 * hops)]
    scratch += tiles(nblk)
    scratch += tiles(*twice[:2])
    scratch += tiles(*twice[:-2])
    scratch += tiles(2 * capacity[-1])
    scratch += [vmem((planes, CHUNKS, n, SLOTS, *tile), bf16) for n in (NX - 1, NX, NX - 1)]
    scratch += [vmem((2 * CHUNKS * sum(capacity), *tile), bf16)]
    scratch += tiles(*[count + CELLS for count in arrived_slots(capacity) for _ in range(2)])
    scratch += tiles(CELLS)
    scratch += tiles(2 * capacity[0] + CELLS)
    stages = (planes * NX * tensors).bit_length() - 1
    scratch += [vmem((2 * stages + 1, 8, 128), f32)]
    scratch += [dma((4,))]
    scratch += [dma((1,)), dma((hops, 2, CHUNKS))]
    scratch += [dma((1,)), dma((planes, CHUNKS))] * 2
    scratch += [dma((1,)), dma((hops, 2, CHUNKS))]
    scratch += [dma((stages,))] * 2
    body = functools.partial(kernel, planes, nblk, capacity)
    in_vmem = pl.BlockSpec(memory_space=pltpu.VMEM)
    return pl.pallas_call(
        body,
        out_shape=(
            jax.ShapeDtypeStruct(grad.shape, bf16),
            jax.ShapeDtypeStruct((1, 1), f32),
        ),
        in_specs=[
            pl.BlockSpec(memory_space=pl.ANY),
            pl.BlockSpec(memory_space=pl.ANY),
            pl.BlockSpec(memory_space=pl.ANY),
            pl.BlockSpec(memory_space=pl.ANY),
        ],
        out_specs=(in_vmem, pl.BlockSpec(memory_space=pltpu.SMEM)),
        scratch_shapes=scratch,
        compiler_params=pltpu.CompilerParams(
            collective_id=number, has_side_effects=True, vmem_limit_bytes=50 * 1024 * 1024
        ),
        cost_estimate=pl.CostEstimate(
            flops=4 * SLOTS * rows * rows * BLK, bytes_accessed=4 * 1024 * 1024, transcendentals=0
        ),
        name=f"sorted_ring_{number}",
    )(table, grad, left_root, right_root)


def precondition(block, left_factor, right_factor):
    left_part = jnp.dot(left_factor, block, preferred_element_type=jnp.float32).astype(jnp.bfloat16)
    product = jnp.dot(left_part, right_factor, preferred_element_type=jnp.float32)
    grad_mean = jnp.mean(jnp.square(block.astype(jnp.float32)))
    prod_mean = jnp.mean(jnp.square(product))
    update = product * (jnp.sqrt(grad_mean + EPSILON) / jnp.sqrt(prod_mean + EPSILON))
    return (update, jnp.sum(update * update))


def padded_call(grad, cell, left_root, right_root, dp_size):
    row_blocks, piece_rows, width = grad.shape
    col_blocks = width // BLK
    per_group = row_blocks * col_blocks
    position = (cell % SLOTS) * dp_size + cell // SLOTS
    select = (position[None, :] == jnp.arange(SLOTS * dp_size, dtype=jnp.int32)[:, None]).astype(jnp.bfloat16)
    pieces = (
        grad.reshape(row_blocks, piece_rows, col_blocks, BLK)
        .transpose(0, 2, 1, 3)
        .reshape(per_group, piece_rows * BLK)
    )
    outgoing = jnp.dot(select, pieces, preferred_element_type=jnp.float32).astype(jnp.bfloat16)
    outgoing = outgoing.reshape(SLOTS, dp_size * piece_rows, BLK)
    arrived = lax.all_to_all(outgoing, "dp", split_axis=1, concat_axis=1, tiled=True)
    outcomes = [precondition(arrived[s], left_root[0, s], right_root[0, s]) for s in range(SLOTS)]
    updates = jnp.stack([outcome[0] for outcome in outcomes]).astype(jnp.bfloat16)
    partial_sum = sum([outcome[1] for outcome in outcomes])
    returned = lax.all_to_all(updates, "dp", split_axis=1, concat_axis=1, tiled=True)
    placed = jnp.take(returned.reshape(SLOTS * dp_size, piece_rows * BLK), position, axis=0)
    placed = placed.reshape(row_blocks, col_blocks, piece_rows, BLK).transpose(0, 2, 1, 3)
    cells = per_group * dp_size * piece_rows * BLK * lax.axis_size("tensor")
    update_rms = jnp.sqrt(lax.psum(partial_sum, ("dp", "tensor")) / cells + EPSILON)
    direction = placed.reshape(row_blocks, piece_rows, width).astype(jnp.float32) * (1.0 / update_rms)
    return direction.astype(jnp.bfloat16), update_rms


def per_device(capacities, grad, owner, left_root, right_root):
    row_blocks, piece_rows, width = grad.shape
    dp_size = lax.axis_size("dp")
    tensors = lax.axis_size("tensor")
    planes = dp_size // NX
    col_blocks = width // BLK
    tensor_index = lax.axis_index("tensor")
    here = lax.dynamic_slice_in_dim(owner, tensor_index * col_blocks, col_blocks, 1).reshape(-1)
    ends, ups, level = plane_split(owner, tensors, planes, capacities)
    cell, rank = block_cells(here)
    ends = lax.dynamic_index_in_dim(ends, tensor_index, 0, keepdims=False)
    ups = lax.dynamic_index_in_dim(ups, tensor_index, 0, keepdims=False)
    table = make_table(cell, rank, ends, ups, dp_size)

    def sorted_lists(number, grad, table, cell, left_root, right_root):
        moved, rms = ring_call(grad, table, left_root, right_root, planes, tensors, capacities[number], number)
        return moved, rms.reshape(())

    def padded(grad, table, cell, left_root, right_root):
        return padded_call(grad, cell, left_root, right_root, dp_size)

    branches = [functools.partial(sorted_lists, number) for number in range(len(capacities))] + [padded]
    return lax.switch(level, branches, grad, table, cell, left_root, right_root)


def build(mesh, capacities):
    return jax.shard_map(
        functools.partial(per_device, capacities),
        mesh=mesh,
        in_specs=(
            P(None, "dp", "tensor"),
            P(),
            P("tensor", "dp", None, None),
            P("tensor", "dp", None, None),
        ),
        out_specs=(P(None, "dp", "tensor"), P()),
        check_vma=False,
    )


def solution(mesh):
    return build(mesh, CAPACITIES)
```

```python
import functools

import jax
import jax.numpy as jnp
from jax import lax
from jax.experimental import pallas as pl
from jax.experimental.pallas import tpu as pltpu
from jax.sharding import PartitionSpec as P

BLK = 512
EPSILON = 1e-06
MESH = pl.DeviceIdType.MESH

NX = 4
SLOTS = 3
CELLS = NX * SLOTS
CHUNKS = 2
BITS = (1, 2, 4, 8, 16, 32)
CAPACITIES = ((38, 34, 30, 25, 20, 15, 10, 5), (42, 37, 34, 28, 24, 19, 12, 7))


def block_cells(owners):
    n = owners.shape[0]
    index = jnp.arange(n, dtype=jnp.int32)
    same = owners[:, None] == owners[None, :]
    slot = jnp.sum((same & (index[None, :] < index[:, None])).astype(jnp.int32), axis=1)
    cell = owners * SLOTS + slot
    rank = jnp.sum((cell[None, :] < cell[:, None]).astype(jnp.int32), axis=1)
    return cell, rank


def plane_split(owner, tensors, planes, capacities):
    z = jnp.arange(planes, dtype=jnp.int32)
    counts = jnp.sum((owner[:, :, None] // NX == z).astype(jnp.float32), axis=0)
    counts = jnp.sum(counts.reshape(tensors, -1, planes), axis=1)
    q = jnp.arange(2 * planes + 1, dtype=jnp.int32)
    turns = (z[:, None] < q[None, :]).astype(jnp.float32) + (z[:, None] + planes < q[None, :]).astype(jnp.float32)
    below = jnp.dot(counts, turns, precision=lax.Precision.HIGHEST).astype(jnp.int32)
    first = below[:, 1 : planes + 1]
    level = jnp.full_like(first, len(capacities))
    ends = first
    for i, capacity in reversed(list(enumerate(capacities))):
        high, low = None, None
        for k, room in enumerate(tuple(capacity) + (0,), 1):
            up = below[:, k : k + planes] + room
            down = below[:, planes + 1 - k : 2 * planes + 1 - k] - room
            high = up if high is None else jnp.minimum(high, up)
            low = down if low is None else jnp.maximum(low, down)
        fits = low <= high
        level = jnp.where(fits, i, level)
        ends = jnp.where(fits, jnp.maximum((high + low) // 2, first), ends)
    return ends, jnp.max(level)


def make_table(cell, rank, ends, devices):
    n = cell.shape[0]
    index = jnp.arange(n, dtype=jnp.int32)
    hit = (rank[None, :] == index[:, None]).astype(jnp.int32)
    block_of = jnp.sum(hit * index[None, :], axis=-1)
    cell_of = jnp.sum(hit * cell[None, :], axis=-1)
    cells = jnp.arange(devices * SLOTS + 1, dtype=jnp.int32)
    below = jnp.sum((cell[None, :] < cells[:, None]).astype(jnp.int32), axis=-1)
    return jnp.concatenate([block_of, cell_of, rank, below, ends])


def fold(piece):
    return jnp.concatenate([piece[:, :128], piece[:, 128:]], axis=0).astype(jnp.bfloat16)


def loop(count, body, unroll):
    turns = count // unroll

    def turn(t, carry):
        for u in range(unroll):
            body(t * unroll + u)
        return carry

    if turns:
        lax.fori_loop(0, turns, turn, 0)
    for j in range(turns * unroll, count):
        body(j)


def arrived_slots(capacity):
    return capacity[1:-2] + (capacity[-2] + capacity[-1], 0)


def kernel(planes, nblk, capacity, *refs):
    hops = len(capacity)
    arrivals = arrived_slots(capacity)
    names = iter(refs)

    def take(*shape):
        if not shape:
            return next(names)
        return [take(*shape[1:]) for _ in range(shape[0])]

    tab_hbm, grad_hbm, left_hbm, right_hbm = take(4)
    out, rms_out = take(2)
    tab, grad, left, right, mats, halves, prods, scales, squares = take(9)
    folded = take(CHUNKS)
    first = take(2, CHUNKS)
    ring = take(hops - 1, 2, CHUNKS)
    ring_last = take(CHUNKS)
    xs, xr, ys = take(3)
    back_send = take()
    back = take(hops - 1, 2, CHUNKS)
    back_first = take(CHUNKS)
    back_last = take(CHUNKS)
    sums = take()
    load_sem, ring_ss, ring_rs, x_ss, x_rs, y_ss, y_rs, back_ss, back_rs, sum_ss, sum_rs = take(11)

    rows = mats.shape[1]
    dp = lax.axis_index("dp")
    tensor = lax.axis_index("tensor")
    tensors = lax.axis_size("tensor")
    z, x = dp // NX, dp % NX
    devices = planes * NX
    per_row = nblk // grad.shape[0]
    CELL_OF, RANK_OF, BELOW = nblk, 2 * nblk, 3 * nblk
    ENDS = BELOW + devices * SLOTS + 1

    def plane(delta):
        return (z + (delta + planes)) % planes

    def device(zz, xx):
        return (zz * NX + xx, tensor)

    toward = [device(plane(1), x), device(plane(-1), x)]
    toward_two = [device(plane(2), x), device(plane(-2), x)]
    along = [None] + [device(z, (x + rel) % NX) for rel in range(1, NX)]

    factors = [
        pltpu.make_async_copy(left_hbm.at[0], left, load_sem.at[0]),
        pltpu.make_async_copy(right_hbm.at[0], right, load_sem.at[1]),
    ]
    inputs = [
        pltpu.make_async_copy(tab_hbm, tab, load_sem.at[2]),
        pltpu.make_async_copy(grad_hbm, grad, load_sem.at[3]),
    ]
    for copy in inputs + factors:
        copy.start()

    barrier = pltpu.get_barrier_semaphore()
    partners = []
    bits = [(place, stride) for place, size in ((0, tensors), (1, devices)) for stride in BITS if stride < size]
    for place, stride in reversed(bits):
        if place:
            partners.append((dp + stride - 2 * stride * ((dp // stride) % 2), tensor))
        else:
            partners.append((dp, tensor + stride - 2 * stride * ((tensor // stride) % 2)))
    peers = toward + along[1:] + [partner for partner in partners if partner[0] is dp]
    for peer in peers:
        pl.semaphore_signal(barrier, inc=1, device_id=peer, device_id_type=MESH)

    for copy in inputs:
        copy.wait()
    end = tab[ENDS + z]

    def fill_chunk(h):
        def fold_row(r):
            for c in range(per_row):
                piece = grad[r, :, pl.ds(c * BLK + h * 256, 256)].astype(jnp.float32)
                folded[h][r * per_row + c] = fold(piece)

        def fill_first(j):
            first[0][h][j] = folded[h][tab[(end - 1 - j) & (nblk - 1)]]
            first[1][h][j] = folded[h][tab[(end + j) & (nblk - 1)]]

        loop(grad.shape[0], fold_row, 4)
        loop(capacity[0], fill_first, 8)

    fill_chunk(0)
    pl.semaphore_wait(barrier, len(peers))

    sends = []

    def describe(src, dst, ss, rs, target):
        return pltpu.make_async_remote_copy(
            src_ref=src, dst_ref=dst, send_sem=ss, recv_sem=rs, device_id=target, device_id_type=MESH
        )

    def start(*args):
        copy = describe(*args)
        copy.start()
        return copy

    def remote(*args):
        copy = start(*args)
        sends.append(copy)
        return copy

    ring_copies = {}

    def ring_at(k, d, h):
        if k < hops:
            return ring[k - 1][d][h]
        return ring_last[h].at[pl.ds(d * capacity[k - 1], capacity[k - 1])]

    def send_ring(k, d, h):
        last = k == hops
        src = first[d][h] if k == 1 else ring_at(k - 2 if last else k - 1, d, h).at[pl.ds(0, capacity[k - 1])]
        target = toward_two[d] if last else toward[d]
        ring_copies[k, d, h] = start(src, ring_at(k, d, h), ring_ss.at[0], ring_rs.at[k - 1, d, h], target)

    for h in range(CHUNKS):
        if h:
            fill_chunk(h)
        for d in range(2):
            send_ring(1, d, h)

    def send_x(delta, h):
        for rel in range(1, NX):
            start(xs.at[delta, h, rel - 1], xr.at[delta, h, rel], x_ss.at[0], x_rs.at[delta, h], along[rel])

    def put_x(delta, h, rel, s, value):
        if rel == 0:
            xr[delta, h, 0, s] = value
        else:
            xs[delta, h, rel - 1, s] = value

    def cell_index(rel, s):
        return z * CELLS + ((x + rel) % NX) * SLOTS + s

    for rel in range(NX):
        for s in range(SLOTS):
            rank = tab[BELOW + cell_index(rel, s)]
            block = tab[jnp.minimum(rank, nblk - 1)]
            for h in range(CHUNKS):
                put_x(0, h, rel, s, folded[h][block])
    for h in range(CHUNKS):
        send_x(0, h)

    def pick(delta, h):
        source = plane(-delta)
        source_end = tab[ENDS + source]
        source_ups = source_end - tab[BELOW + (source + 1) * CELLS]
        k = min(delta, planes - delta)
        room = capacity[k - 1]
        for rel in range(NX):
            for s in range(SLOTS):
                rank = tab[BELOW + cell_index(rel, s)]
                up = (source_end - 1 - rank) & (nblk - 1)
                down = (rank - source_end) & (nblk - 1)
                if k == hops:
                    at = jnp.where(up < source_ups, jnp.minimum(up, room - 1), room + jnp.minimum(down, room - 1))
                    value = ring_last[h][at]
                elif delta < hops:
                    value = ring[k - 1][0][h][jnp.minimum(up, room - 1)]
                else:
                    value = ring[k - 1][1][h][jnp.minimum(down, room - 1)]
                put_x(delta, h, rel, s, value)
        send_x(delta, h)

    squares[...] = jnp.zeros_like(squares)

    def place(delta, h):
        arrived = xr.at[delta, h, pl.ds(1, NX - 1)]
        describe(arrived, arrived, x_ss.at[0], x_rs.at[delta, h], along[1]).wait_recv()
        source = plane(-delta)
        for s in range(SLOTS):
            total = None
            for pair in range(NX // 2):
                low, high = (
                    xr[delta, h, (x - (2 * pair + i) + NX) % NX, s].astype(jnp.float32) for i in range(2)
                )
                term = low * low + high * high
                total = term if total is None else total + term
                at = pl.ds(pl.multiple_of(source * (8 * NX) + 16 * pair, 16), 16)
                mats[s, at, pl.ds(h * 256, 128)] = jnp.concatenate([low[:8], high[:8]], 0).astype(jnp.bfloat16)
                mats[s, at, pl.ds(h * 256 + 128, 128)] = jnp.concatenate([low[8:], high[8:]], 0).astype(jnp.bfloat16)
            squares[s] += total

    pending = [(0, h) for h in range(CHUNKS)]
    for k in range(1, hops + 1):
        for h in range(CHUNKS):
            for d in range(2):
                ring_copies[k, d, h].wait_recv()
                if k < hops - 1:
                    send_ring(k + 1, d, h)
                if k == hops - 2:
                    send_ring(hops, d, h)
            ready = []
            for delta in sorted({k, planes - k}):
                ready.append((delta, h))
            for delta, hh in ready:
                pick(delta, hh)
            while len(pending) > 4:
                place(*pending.pop(0))
            pending += ready
    for copy in factors:
        copy.wait()
    for h in range(CHUNKS):
        for item in [p for p in pending if p[1] == h]:
            place(*item)

        def left_part(s, carry):
            part = jnp.dot(left[s], mats[s, :, pl.ds(h * 256, 256)], preferred_element_type=jnp.float32)
            halves[s, :, pl.ds(h * 256, 256)] = part.astype(jnp.bfloat16)
            return carry

        for s in range(SLOTS):
            left_part(s, 0)

    cells = rows * BLK

    def right_part(s, total):
        product = jnp.dot(halves[s], right[s], preferred_element_type=jnp.float32)
        prods[s] = product
        prod_sum = jnp.sum(product * product, keepdims=True)
        grad_sum = jnp.sum(squares[s], keepdims=True)
        scale = jnp.sqrt(grad_sum / cells + EPSILON) / jnp.sqrt(prod_sum / cells + EPSILON)
        scales[s] = jnp.broadcast_to(scale, (8, 128))
        own = tab[BELOW + dp * SLOTS + s]
        found = jnp.full((1, 1), tab[CELL_OF + jnp.minimum(own, nblk - 1)])
        held = found == jnp.full((1, 1), dp * SLOTS + s)
        return total + jnp.where(held, prod_sum * scale * scale, 0.0)

    total = jnp.zeros((1, 1), jnp.float32)
    for s in range(SLOTS):
        total = right_part(s, total)
    stages = len(partners)
    sums[0] = jnp.broadcast_to(total, sums.shape[1:])
    sum_copies = []

    def exchange():
        i = len(sum_copies)
        if i:
            sum_copies[i - 1].wait_recv()
            sums[2 * i] = sums[2 * i - 2] + sums[2 * i - 1]
        if i < stages:
            sum_copies.append(
                remote(sums.at[2 * i], sums.at[2 * i + 1], sum_ss.at[i], sum_rs.at[i], partners[i])
            )


    def y_at(delta, h):
        if delta == 0:
            return back_last[h], 2 * capacity[0]
        if delta == hops:
            return back_first[h], 0
        k, d = (delta, 1) if delta < hops else (planes - delta, 0)
        return back[k - 1][d][h], arrivals[k - 1]

    def send_y(delta):
        target = plane(delta)
        for s in range(SLOTS):
            scale = scales[s][:, :1]
            for rel in range(NX):
                xx = (x + rel) % NX
                value = prods[s, pl.ds(pl.multiple_of((target * NX + xx) * 8, 8), 8), :] * scale
                for h in range(CHUNKS):
                    part = fold(value[:, h * 256 : (h + 1) * 256])
                    if rel == 0:
                        ref, row = y_at(delta, h)
                        ref[row + x * SLOTS + s] = part
                    else:
                        ys[delta, h, rel - 1, s] = part
        for h in range(CHUNKS):
            ref, row = y_at(delta, h)
            for rel in range(1, NX):
                landing = ref.at[pl.ds(row + x * SLOTS, SLOTS)]
                start(ys.at[delta, h, rel - 1], landing, y_ss.at[0], y_rs.at[delta, h], along[rel])

    waited = set()

    def wait_y(delta, h):
        if (delta, h) not in waited:
            waited.add((delta, h))
            alike = ys.at[delta, h]
            describe(alike, alike, y_ss.at[0], y_rs.at[delta, h], along[1]).wait_recv()

    back_copies = {}
    cells_all = planes * CELLS

    def send_back(k, d, h):
        for farther in [k + 1] * (k < hops - 1) + [hops] * (k == hops - 2):
            back_copies[farther, d, h].wait_recv()
        delta = planes - k if d == 0 else k
        wait_y(delta, h)
        target_end = tab[ENDS + plane(delta)]
        low = z * CELLS
        width = capacity[k - 1]
        filled = capacity[k] if k < hops - 1 else 0
        ref, row = y_at(delta, h)
        offset = sum(capacity[: k - 1]) * 2 * CHUNKS + (d * CHUNKS + h) * width

        def merge(j, keep):
            rank = (target_end - 1 - j if d == 0 else target_end + j) & (nblk - 1)
            local = tab[CELL_OF + rank] - low
            at = row + jnp.clip(local, 0, CELLS - 1)
            if keep:
                other = j
                if k == hops - 2:
                    away = lax.rem(local + cells_all, cells_all)
                    away = away - 2 * CELLS if d == 0 else cells_all - 1 - away - CELLS
                    two = (away >= 0) & (away < CELLS)
                    other = jnp.where(two, filled + jnp.minimum(j, capacity[k + 1] - 1), j)
                at = jnp.where((local >= 0) & (local < CELLS), at, other)
            back_send[offset + j] = ref[at]

        loop(filled, functools.partial(merge, keep=True), 8)
        loop(width - filled, lambda j: merge(filled + j, False), 8)
        if k == hops:
            landing = back[k - 3][d][h].at[pl.ds(capacity[k - 2], width)]
        elif k > 1:
            landing = back[k - 2][d][h].at[pl.ds(0, width)]
        else:
            landing = back_last[h].at[pl.ds(d * width, width)]
        target = toward_two[1 - d] if k == hops else toward[1 - d]
        source = back_send.at[pl.ds(offset, width)]
        back_copies[k, d, h] = start(source, landing, back_ss.at[0], back_rs.at[k - 1, d, h], target)

    points = [(hops, 0)] + [(k, 1) for k in range(hops - 2, max(hops - 5, 0), -1)]
    points += [(k, h) for k in range(hops - 5, 0, -1) for h in range(CHUNKS)]
    points = points[:stages]
    sent = set()

    def ensure_y(delta):
        if delta not in sent:
            sent.add(delta)
            send_y(delta)

    for k in range(hops, 0, -1):
        for ahead in range(k, max(k - 3, -1), -1):
            ensure_y((planes - ahead) % planes)
            ensure_y(ahead)
        for h in range(CHUNKS):
            for d in range(2):
                send_back(k, d, h)
            if (k, h) in points:
                exchange()
    ensure_y(0)
    while len(sum_copies) < stages:
        exchange()
    exchange()
    update_rms = jnp.sqrt(sums[2 * stages] / (nblk * cells * tensors) + EPSILON)
    rms_out[0, 0] = update_rms[0, 0]
    inv_rms = (1.0 / update_rms)[:1, :1]

    end = tab[ENDS + z]
    ups = end - tab[BELOW + (z + 1) * CELLS]
    for h in range(CHUNKS):
        for d in range(2):
            back_copies[1, d, h].wait_recv()
        wait_y(0, h)

        def finish(b, h=h):
            rank = tab[RANK_OF + b]
            local = tab[CELL_OF + rank] - z * CELLS
            up = (end - 1 - rank) & (nblk - 1)
            down = (rank - end) & (nblk - 1)
            room = capacity[0]
            at = jnp.where(up < ups, jnp.minimum(up, room - 1), room + jnp.minimum(down, room - 1))
            mine = (local >= 0) & (local < CELLS)
            at = jnp.where(mine, 2 * room + jnp.clip(local, 0, CELLS - 1), at)
            value = back_last[h][at].astype(jnp.float32) * inv_rms
            wide = jnp.concatenate([value[:8], value[8:]], axis=1).astype(jnp.bfloat16)
            column = (b % per_row) * BLK + h * 256
            out[b // per_row, :, pl.ds(pl.multiple_of(column, 256), 256)] = wide

        loop(nblk, finish, 16)

    for copy in sends:
        copy.wait_send()
    describe(xs, xs, x_ss.at[0], x_rs.at[0, 0], along[1]).wait_send()
    describe(ys, ys, y_ss.at[0], y_rs.at[0, 0], along[1]).wait_send()
    describe(back_send, back_send, ring_ss.at[0], ring_rs.at[0, 0, 0], toward[0]).wait_send()
    describe(back_send, back_send, back_ss.at[0], back_rs.at[0, 0, 0], toward[0]).wait_send()


def ring_call(grad, table, left_root, right_root, planes, tensors, capacity, number):
    row_blocks, piece_rows, width = grad.shape
    nblk = row_blocks * (width // BLK)
    rows = left_root.shape[-1]
    hops = len(capacity)
    tile = (16, 128)
    bf16, f32 = jnp.bfloat16, jnp.float32
    vmem = pltpu.VMEM
    dma = pltpu.SemaphoreType.DMA

    def tiles(*counts):
        return [vmem((count, *tile), bf16) for count in counts for _ in range(CHUNKS)]

    scratch = [
        pltpu.SMEM(table.shape, jnp.int32),
        vmem(grad.shape, bf16),
        vmem((SLOTS, rows, rows), bf16),
        vmem((SLOTS, BLK, BLK), bf16),
        vmem((SLOTS, rows, BLK), bf16),
        vmem((SLOTS, rows, BLK), bf16),
        vmem((SLOTS, rows, BLK), f32),
        vmem((SLOTS, 8, 128), f32),
        vmem((SLOTS, *tile), f32),
    ]
    twice = [capacity[k // 2] for k in range(2 * hops)]
    scratch += tiles(nblk)
    scratch += tiles(*twice[:2])
    scratch += tiles(*twice[:-2])
    scratch += tiles(2 * capacity[-1])
    scratch += [vmem((planes, CHUNKS, n, SLOTS, *tile), bf16) for n in (NX - 1, NX, NX - 1)]
    scratch += [vmem((2 * CHUNKS * sum(capacity), *tile), bf16)]
    scratch += tiles(*[count + CELLS for count in arrived_slots(capacity) for _ in range(2)])
    scratch += tiles(CELLS)
    scratch += tiles(2 * capacity[0] + CELLS)
    stages = (planes * NX * tensors).bit_length() - 1
    scratch += [vmem((2 * stages + 1, 8, 128), f32)]
    scratch += [dma((4,))]
    scratch += [dma((1,)), dma((hops, 2, CHUNKS))]
    scratch += [dma((1,)), dma((planes, CHUNKS))] * 2
    scratch += [dma((1,)), dma((hops, 2, CHUNKS))]
    scratch += [dma((stages,))] * 2
    body = functools.partial(kernel, planes, nblk, capacity)
    in_vmem = pl.BlockSpec(memory_space=pltpu.VMEM)
    return pl.pallas_call(
        body,
        out_shape=(
            jax.ShapeDtypeStruct(grad.shape, bf16),
            jax.ShapeDtypeStruct((1, 1), f32),
        ),
        in_specs=[
            pl.BlockSpec(memory_space=pl.ANY),
            pl.BlockSpec(memory_space=pl.ANY),
            pl.BlockSpec(memory_space=pl.ANY),
            pl.BlockSpec(memory_space=pl.ANY),
        ],
        out_specs=(in_vmem, pl.BlockSpec(memory_space=pltpu.SMEM)),
        scratch_shapes=scratch,
        compiler_params=pltpu.CompilerParams(
            collective_id=number, has_side_effects=True, vmem_limit_bytes=50 * 1024 * 1024
        ),
        cost_estimate=pl.CostEstimate(
            flops=4 * SLOTS * rows * rows * BLK, bytes_accessed=4 * 1024 * 1024, transcendentals=0
        ),
        name=f"sorted_ring_{number}",
    )(table, grad, left_root, right_root)


def precondition(block, left_factor, right_factor):
    left_part = jnp.dot(left_factor, block, preferred_element_type=jnp.float32).astype(jnp.bfloat16)
    product = jnp.dot(left_part, right_factor, preferred_element_type=jnp.float32)
    grad_mean = jnp.mean(jnp.square(block.astype(jnp.float32)))
    prod_mean = jnp.mean(jnp.square(product))
    update = product * (jnp.sqrt(grad_mean + EPSILON) / jnp.sqrt(prod_mean + EPSILON))
    return (update, jnp.sum(update * update))


def padded_call(grad, cell, left_root, right_root, dp_size):
    row_blocks, piece_rows, width = grad.shape
    col_blocks = width // BLK
    per_group = row_blocks * col_blocks
    position = (cell % SLOTS) * dp_size + cell // SLOTS
    select = (position[None, :] == jnp.arange(SLOTS * dp_size, dtype=jnp.int32)[:, None]).astype(jnp.bfloat16)
    pieces = (
        grad.reshape(row_blocks, piece_rows, col_blocks, BLK)
        .transpose(0, 2, 1, 3)
        .reshape(per_group, piece_rows * BLK)
    )
    outgoing = jnp.dot(select, pieces, preferred_element_type=jnp.float32).astype(jnp.bfloat16)
    outgoing = outgoing.reshape(SLOTS, dp_size * piece_rows, BLK)
    arrived = lax.all_to_all(outgoing, "dp", split_axis=1, concat_axis=1, tiled=True)
    outcomes = [precondition(arrived[s], left_root[0, s], right_root[0, s]) for s in range(SLOTS)]
    updates = jnp.stack([outcome[0] for outcome in outcomes]).astype(jnp.bfloat16)
    partial_sum = sum([outcome[1] for outcome in outcomes])
    returned = lax.all_to_all(updates, "dp", split_axis=1, concat_axis=1, tiled=True)
    placed = jnp.take(returned.reshape(SLOTS * dp_size, piece_rows * BLK), position, axis=0)
    placed = placed.reshape(row_blocks, col_blocks, piece_rows, BLK).transpose(0, 2, 1, 3)
    cells = per_group * dp_size * piece_rows * BLK * lax.axis_size("tensor")
    update_rms = jnp.sqrt(lax.psum(partial_sum, ("dp", "tensor")) / cells + EPSILON)
    direction = placed.reshape(row_blocks, piece_rows, width).astype(jnp.float32) * (1.0 / update_rms)
    return direction.astype(jnp.bfloat16), update_rms


def per_device(capacities, grad, owner, left_root, right_root):
    row_blocks, piece_rows, width = grad.shape
    dp_size = lax.axis_size("dp")
    tensors = lax.axis_size("tensor")
    planes = dp_size // NX
    col_blocks = width // BLK
    tensor_index = lax.axis_index("tensor")
    here = lax.dynamic_slice_in_dim(owner, tensor_index * col_blocks, col_blocks, 1).reshape(-1)
    ends, level = plane_split(owner, tensors, planes, capacities)
    cell, rank = block_cells(here)
    ends = lax.dynamic_index_in_dim(ends, tensor_index, 0, keepdims=False)
    table = make_table(cell, rank, ends, dp_size)

    def sorted_lists(number, grad, table, cell, left_root, right_root):
        moved, rms = ring_call(grad, table, left_root, right_root, planes, tensors, capacities[number], number)
        return moved, rms.reshape(())

    def padded(grad, table, cell, left_root, right_root):
        return padded_call(grad, cell, left_root, right_root, dp_size)

    branches = [functools.partial(sorted_lists, number) for number in range(len(capacities))] + [padded]
    return lax.switch(level, branches, grad, table, cell, left_root, right_root)


def build(mesh, capacities):
    return jax.shard_map(
        functools.partial(per_device, capacities),
        mesh=mesh,
        in_specs=(
            P(None, "dp", "tensor"),
            P(),
            P("tensor", "dp", None, None),
            P("tensor", "dp", None, None),
        ),
        out_specs=(P(None, "dp", "tensor"), P()),
        check_vma=False,
    )


def solution(mesh):
    return build(mesh, CAPACITIES)
```
